32 devices in a mesh: obs: 4 (over x, core), par: 8 (over z, y).
Axes of the slice: x: 2, y: 2, z: 4, core: 2. Of those that a mesh axis runs over, the one named last changes fastest.
Arguments:
- blocks: bfloat16 [4096, 128, 128], P(('obs', 'par')), may hold values from -0.046875 to 0.046875
- owner: int32 [4096, 1], P(('obs', 'par')), may hold values from 0 to 31; in each aligned block of 128 rows (0 to 127, 128 to 255, ...) at most 8 rows name the same one
- row_local: int32 [4096], P(('obs', 'par')), may hold values from 0 to 31
- col_local: int32 [4096], P(('obs', 'par')), may hold values from 0 to 7
- sketch: bfloat16 [8192, 512], P('par'), may hold values from -6 to 6
Outputs:
- basis: bfloat16 [16384, 512], P(('obs', 'par'))
- projected: float32 [512, 8192], P('obs', 'par')
The draws below stay inside these ranges and needn't reach their ends.
Inputs may be any that keep to these rules, and one draw needn't show every extreme that they name: The blocks of one device name at most 8 times the same owner; in every draw some device names some owner exactly 8 times, and every owner is named by some block.
All inputs are finite; a program needn't handle non-finite values.
Results may differ from the reference program's by a relative error of at most 0.015.
Values may be sent and summed in bfloat16 or wider, within the bound.
No kernel may reach another device: no remote copies, remote signals or barrier semaphores. Data moves between devices by JAX's collectives and lax.ppermute only.
A program may use at most 128 MiB of HBM per device.

```python
import math
import jax
import jax.numpy as jnp
import numpy as np
from jax import lax

BS = 128
K = 512
RB_DEV = 32
CB_DEV = 8
BLK_DEV = 128
CAP = 8
NOBS = 16384
NPAR = 8192
BLOCKS = 4096
N_PAR = 8
DEVICES = 32


def with_ends(drawn, own_key, low, top_value):
    extent = drawn.shape
    spot = [jax.random.randint(jax.random.fold_in(own_key, axis), (), 0, extent[axis]) for axis in range(len(extent))]
    drawn = drawn.at[tuple(spot)].set(low)
    longest = extent.index(max(extent))
    spot[longest] = (spot[longest] + 1) % extent[longest]
    return drawn.at[tuple(spot)].set(top_value)


def steps_of(stream_key, shape, split, least, largest):
    def one(axis_at, parts):
        heights = jax.random.uniform(jax.random.fold_in(jax.random.fold_in(stream_key, 6), axis_at), (parts,), jnp.float32, least / len(split), largest / len(split))
        return jnp.repeat(jnp.exp(heights), shape[axis_at] // parts).reshape((-1,) + (1,) * (len(shape) - axis_at - 1))

    level = one(*split[0])
    for cut in split[1:]:
        level = level * one(*cut)
    return level


def deal_out(rng, own, number, rows, number_of, top, bound, skew):
    ranking = jax.random.permutation(rng, number_of)
    packed, ordinary = shares(number_of, rows * top, bound, skew, True), shares(number_of, rows * top, bound, skew, False)
    places = jnp.arange(number_of)

    def named(lengths, rotation):
        used = int((lengths > 0).sum())
        fixed = max(1, used // 4)
        moved = fixed + (places - fixed + rotation * (used - fixed)) % max(1, number_of - fixed)
        return jnp.zeros((number_of,), jnp.int32).at[ranking[jnp.where(places < fixed, places, moved)]].set(jnp.asarray(lengths, jnp.int32))

    lengths = jnp.where(number % 4 == 0, named(packed, number // 4), named(ordinary, number - number // 4 - 1))
    mixed = jax.random.permutation(jax.random.fold_in(own, 3), number_of)
    giver, sink = mixed[0:number_of // 2 * 2:2], mixed[1:number_of // 2 * 2:2]
    slack = jnp.minimum(lengths[giver] - 1, bound - lengths[sink]) // 2
    slack = jnp.where((giver == ranking[0]) | (sink == ranking[0]) | (lengths[sink] == 0), 0, jnp.maximum(slack, 0))
    moved = jax.random.randint(jax.random.fold_in(own, 4), (number_of // 2,), 0, 1 << 20) % (slack + 1)
    lengths = lengths.at[giver].add(-moved).at[sink].add(moved)
    members = jnp.searchsorted(jnp.cumsum(lengths), jnp.arange(rows * top), side="right").astype(jnp.int32)
    grid = members.reshape(top, rows).T
    grid = grid[jax.random.permutation(jax.random.fold_in(own, 1), rows)]
    rotation = jax.random.randint(jax.random.fold_in(own, 2), (rows, 1), 0, top)
    return jnp.take_along_axis(grid, (jnp.arange(top)[None, :] + rotation) % top, axis=1)


def shares(amount, total, reach, slope, full):
    weights = [(1 << 20) // math.isqrt(grade ** slope) + 1 for grade in range(1, amount + 1)]
    largest = reach if full else min(reach, max(-(-total // amount), total * weights[0] // sum(weights)))
    least = 1 if total - largest >= amount - 1 else 0
    given, spare = [largest] + [least] * (amount - 1), total - largest - least * (amount - 1)
    while spare > 0:
        free = [i for i in range(1, amount) if given[i] < largest] or [i for i in range(1, amount) if given[i] < reach]
        mass, left = sum([weights[i] for i in free]), spare
        for i in free:
            more = min(reach - given[i], max(1, left * weights[i] // mass), spare)
            given[i] = given[i] + more
            spare = spare - more
    return np.array(given)


def centred(own_key, shape, scale, most, shards=(), kind=jnp.bfloat16):
    factor_of = steps_of(own_key, shape, shards, -0.22, 0.18) if shards else 1.0
    entries = jax.random.normal(own_key, shape, jnp.float32) * scale * factor_of
    return jnp.minimum(jnp.maximum(entries, -most), most).astype(kind)


def setup_inputs(seed: int = 0) -> dict:
    streams_of = jax.random.split(jax.random.key(seed), 6)
    blocks = centred(streams_of[0], (BLOCKS, BS, BS), (BS * BLK_DEV) ** -0.5, 0.046875, ((0, 32),))
    owner_keys = jax.random.split(jax.random.fold_in(streams_of[1], 1), BLOCKS // BLK_DEV)
    owner_turns = jax.random.permutation(jax.random.fold_in(streams_of[1], 3), BLOCKS // BLK_DEV)
    owner = jax.vmap(lambda own, number: deal_out(jax.random.fold_in(streams_of[1], 2), own, number, BLK_DEV, DEVICES, 1, CAP, 2))(owner_keys, owner_turns).reshape((BLOCKS, 1))
    row_local = with_ends(jax.random.randint(streams_of[2], (BLOCKS,), 0, RB_DEV), jax.random.fold_in(streams_of[2], 1), 0, RB_DEV - 1).astype(jnp.int32)
    col_local = with_ends(jax.random.randint(streams_of[3], (BLOCKS,), 0, CB_DEV), jax.random.fold_in(streams_of[3], 1), 0, CB_DEV - 1).astype(jnp.int32)
    sketch = centred(streams_of[4], (NPAR, K), 1.0, 6.0, ((0, 8),))
    return dict(blocks=blocks, owner=owner, row_local=row_local, col_local=col_local, sketch=sketch)


def reference(blocks, owner, row_local, col_local, sketch):
    destination = owner[:, 0]
    row_block = destination // N_PAR * RB_DEV + row_local
    col_block = destination % N_PAR * CB_DEV + col_local
    row_groups = NOBS // BS
    col_groups = NPAR // BS
    sketch_panels = sketch.reshape(col_groups, BS, K)
    grouped = blocks.reshape(DEVICES, BLK_DEV, BS, BS)
    rows_grouped = row_block.reshape(DEVICES, BLK_DEV)
    cols_grouped = col_block.reshape(DEVICES, BLK_DEV)

    def sketch_step(totals, inputs):
        values, row_sel, col_sel = inputs
        product = jnp.einsum('sij,sjk->sik', values.astype(jnp.float32), sketch_panels[col_sel].astype(jnp.float32))
        return (totals.at[row_sel].add(product), None)
    sketched = lax.scan(sketch_step, jnp.zeros((row_groups, BS, K), jnp.float32), (grouped, rows_grouped, cols_grouped))[0]
    sketched = sketched.reshape(NOBS, K)
    gram_matrix = jnp.dot(sketched.T.astype(jnp.float32), sketched.astype(jnp.float32), precision=lax.Precision.HIGHEST, preferred_element_type=jnp.float32) / NOBS
    lower_factor = jnp.linalg.cholesky(gram_matrix)
    basis = jax.scipy.linalg.solve_triangular(lower_factor, sketched.T, lower=True).T.astype(jnp.bfloat16)
    basis_panels = basis.reshape(row_groups, BS, K)

    def project_step(totals, inputs):
        values, row_sel, col_sel = inputs
        product = jnp.einsum('sik,sij->skj', basis_panels[row_sel].astype(jnp.float32), values.astype(jnp.float32))
        return (totals.at[col_sel].add(product), None)
    projected = lax.scan(project_step, jnp.zeros((col_groups, K, BS), jnp.float32), (grouped, rows_grouped, cols_grouped))[0]
    projected = jnp.transpose(projected, (1, 0, 2)).reshape(K, NPAR)
    return (basis, projected)
```

```python
import functools

import jax
import jax.numpy as jnp
from jax import lax
from jax.experimental import pallas as pl
from jax.experimental.pallas import tpu as pltpu
from jax.sharding import Mesh, PartitionSpec as P

RB_DEV = 32
UNROLL = 4
VMEM_LIMIT = 60 * 1024 * 1024
HIGHEST = lax.Precision.HIGHEST
ALL = ("x", "core", "p", "q")


def shift(value, axis, by):
    size = lax.axis_size(axis)
    return lax.ppermute(value, axis, [(i, (i + by) % size) for i in range(size)])


def collect(rows_ref, cols_ref, sources, slots, list_rows, list_cols, sem, spare):
    count = jnp.int32(0)
    base = 0
    for source in sources:
        held = source.shape[0]

        def take(i, count, source=source, base=base):
            row = rows_ref[base + i]

            @pl.when(row >= 0)
            def _():
                pltpu.make_async_copy(source.at[i], slots.at[count], sem).start()
                list_rows[count] = row
                list_cols[count] = cols_ref[base + i]

            return count + jnp.where(row >= 0, 1, 0).astype(jnp.int32)

        count = lax.fori_loop(0, held, take, count)
        base += held
    for extra in range(UNROLL - 1):
        list_rows[count + extra] = spare
        list_cols[count + extra] = 0

    def settle(i, carry):
        pltpu.make_async_copy(sources[0].at[0], slots.at[0], sem).wait()
        return carry

    lax.fori_loop(0, count, settle, 0)
    return count


def sketch_kernel(sources_n, rows_ref, cols_ref, *refs):
    sources, (near, far) = refs[:sources_n], refs[sources_n : sources_n + 2]
    outs, scratch = refs[sources_n + 2 : -7], refs[-7:]
    slots, panels, acc, list_rows, list_cols, sem, panel_sem = scratch
    half = near.shape[0]
    copies = [
        pltpu.make_async_copy(near, panels.at[pl.ds(0, half)], panel_sem.at[0]),
        pltpu.make_async_copy(far, panels.at[pl.ds(half, half)], panel_sem.at[1]),
    ]
    for copy in copies:
        copy.start()
    spare = acc.shape[0] - 1

    def clear(i, carry):
        acc[i] = jnp.zeros(acc.shape[1:], acc.dtype)
        return carry

    lax.fori_loop(0, spare, clear, 0)
    count = collect(rows_ref, cols_ref, sources, slots, list_rows, list_cols, sem, spare)
    for copy in copies:
        copy.wait()

    def step(i, carry):
        for j in range(UNROLL):
            k = i * UNROLL + j
            row = list_rows[k]
            acc[row] += jnp.dot(
                slots[k], panels[list_cols[k]], preferred_element_type=jnp.float32
            )
        return carry

    lax.fori_loop(0, (count + UNROLL - 1) // UNROLL, step, 0)
    width = outs[0].shape[-1]
    chunks = acc.shape[-1] // width
    groups = len(outs) // chunks
    per = spare // groups
    for g in range(groups):

        def give(i, carry, g=g):
            for c in range(chunks):
                out = outs[g * chunks + c]
                out[i] = acc[g * per + i, :, c * width : (c + 1) * width].astype(out.dtype)
            return carry

        lax.fori_loop(0, per, give, 0)


def project_kernel(sources_n, x_n, q_n, rows_ref, cols_ref, *refs):
    sources, (near, far) = refs[:sources_n], refs[sources_n : sources_n + 2]
    outs, scratch = refs[sources_n + 2 : -7], refs[-7:]
    slots, panels, acc, list_rows, list_cols, sem, panel_sem = scratch
    half = near.shape[0]
    copies = [
        pltpu.make_async_copy(near, panels.at[pl.ds(0, half)], panel_sem.at[0]),
        pltpu.make_async_copy(far, panels.at[pl.ds(half, half)], panel_sem.at[1]),
    ]
    for copy in copies:
        copy.start()
    spare = acc.shape[0] - 1

    def clear(i, carry):
        acc[i] = jnp.zeros(acc.shape[1:], acc.dtype)
        return carry

    lax.fori_loop(0, spare, clear, 0)
    count = collect(rows_ref, cols_ref, sources, slots, list_rows, list_cols, sem, spare)
    for copy in copies:
        copy.wait()

    def step(i, carry):
        for j in range(UNROLL):
            k = i * UNROLL + j
            row = list_rows[k]
            acc[row] += lax.dot_general(
                slots[k],
                panels[list_cols[k]],
                (((0,), (0,)), ((), ())),
                preferred_element_type=jnp.float32,
            )
        return carry

    lax.fori_loop(0, (count + UNROLL - 1) // UNROLL, step, 0)
    width = acc.shape[-1] // 2
    inner = spare // (x_n * q_n)
    for g in range(x_n):

        def give_x(i, carry, g=g):
            out = outs[g]
            out[i] = acc[g * q_n * inner + i, :, :width].astype(out.dtype)
            return carry

        lax.fori_loop(0, q_n * inner, give_x, 0)
    for g in range(q_n):
        for x in range(x_n):

            def give_q(i, carry, g=g, x=x):
                out = outs[x_n + g]
                out[x * inner + i] = acc[(x * q_n + g) * inner + i, :, width:].astype(out.dtype)
                return carry

            lax.fori_loop(0, inner, give_q, 0)


def block_products(kernel, rows, cols, sources, near, far, slots_n, acc_n, outs, name):
    wide, width = near.shape[1], near.shape[2]
    smem = pl.BlockSpec(memory_space=pltpu.SMEM)
    anywhere = pl.BlockSpec(memory_space=pl.ANY)
    return pl.pallas_call(
        kernel,
        out_shape=outs,
        in_specs=[smem, smem] + [anywhere] * (len(sources) + 2),
        out_specs=[pl.BlockSpec(memory_space=pltpu.VMEM)] * len(outs),
        scratch_shapes=[
            pltpu.VMEM((slots_n + UNROLL, wide, wide), jnp.bfloat16),
            pltpu.VMEM((2 * near.shape[0], wide, width), jnp.bfloat16),
            pltpu.VMEM((acc_n + 1, wide, width), jnp.float32),
            pltpu.SMEM((slots_n + UNROLL,), jnp.int32),
            pltpu.SMEM((slots_n + UNROLL,), jnp.int32),
            pltpu.SemaphoreType.DMA,
            pltpu.SemaphoreType.DMA((2,)),
        ],
        compiler_params=pltpu.CompilerParams(vmem_limit_bytes=VMEM_LIMIT),
        cost_estimate=pl.CostEstimate(
            flops=2 * 128 * wide * wide * width, bytes_accessed=32 << 20, transcendentals=0
        ),
        name=name,
    )(rows, cols, *sources, near, far)


def absolute(pieces, axis):
    size, me = len(pieces), lax.axis_index(axis)
    laid = jnp.concatenate(pieces + pieces[:-1], axis=0)
    rows = pieces[0].shape[0]
    return lax.dynamic_slice_in_dim(laid, (size - me) % size * rows, size * rows, axis=0)


def reduce_stage(keep, sends, axis):
    total = keep
    for k, part in enumerate(sends, 1):
        total = total + shift(part, axis, k).astype(jnp.float32)
    return total


def per_device(blocks, owner, row_local, col_local, sketch):
    x_n, q_n, p_n = lax.axis_size("x"), lax.axis_size("q"), lax.axis_size("p")
    xi, ci, zi, yi = (lax.axis_index(a) for a in ALL)
    par = p_n * q_n
    total_devs = 2 * x_n * par
    held, wide = blocks.shape[0], blocks.shape[1]
    width = sketch.shape[1]
    col_dev = sketch.shape[0] // wide
    slot_cap = max(2, (2 * held + total_devs - 1) // total_devs)
    rows_each = RB_DEV // par
    cols_each = col_dev // (2 * x_n)
    all_rows = RB_DEV * wide * 2 * x_n
    bf16, f32 = jnp.bfloat16, jnp.float32

    code = (owner[:, 0] * RB_DEV + row_local) * col_dev + col_local
    pair = jnp.concatenate([code, shift(code, "core", 1)])
    codes = [pair] + [shift(pair, "x", k) for k in range(1, x_n)]
    sources = [blocks, shift(blocks, "core", 1)]
    for k in range(1, x_n):
        far_blocks = shift(blocks, "x", k)
        sources += [far_blocks, shift(far_blocks, "core", 1)]
    codes = jnp.concatenate(codes)

    half_rows = sketch.shape[0] // 2
    my_half = lax.dynamic_slice_in_dim(sketch, ci * half_rows, half_rows, axis=0)
    near = lax.all_gather(my_half, ("p", "q"), axis=0, tiled=True)
    far = shift(near, "core", 1)
    panels = (par * col_dev // 2, wide, width)
    near, far = near.reshape(panels), far.reshape(panels)

    owners = codes // (RB_DEV * col_dev)
    row = codes // col_dev % RB_DEV
    col = codes % col_dev
    o_obs, o_par = owners // par, owners % par
    o_x, o_core = o_obs // 2, o_obs % 2
    r_par, r_in = row // rows_each, row % rows_each
    r_z, r_y = r_par // q_n, r_par % q_n
    c_x, c_core, c_in = col // (2 * cols_each), col // cols_each % 2, col % cols_each
    half_cols = col_dev // 2

    y_slot = (((r_y - yi) % q_n) * p_n + (r_z - zi) % p_n) * rows_each + r_in
    y_slot = jnp.where(o_obs == xi * 2 + ci, y_slot, -1)
    y_panel = (
        jnp.where(col // half_cols == ci, 0, par * half_cols)
        + o_par * half_cols
        + col % half_cols
    )
    p_slot = (((c_x - xi) % x_n * q_n + (o_par % q_n - yi) % q_n) * p_n + (o_par // q_n - zi) % p_n)
    p_slot = p_slot * cols_each + c_in
    p_slot = jnp.where((o_x == xi) & (c_core == ci), p_slot, -1)
    p_panel = jnp.where(o_core == ci, 0, RB_DEV) + row

    chunks = 2
    kc = width // chunks
    per = p_n * rows_each
    shapes = [jax.ShapeDtypeStruct((per, wide, kc), f32)] * chunks
    shapes += [jax.ShapeDtypeStruct((per, wide, kc), bf16)] * (chunks * (q_n - 1))
    parts = block_products(
        functools.partial(sketch_kernel, len(sources)),
        y_slot, y_panel, sources, near, far,
        par * slot_cap * 2 * x_n, RB_DEV, shapes, "sketch_products",
    )
    own = []
    for c in range(chunks):
        total = reduce_stage(parts[c], [parts[k * chunks + c] for k in range(1, q_n)], "q")
        total = total.reshape(p_n, rows_each * wide, kc)
        own.append(reduce_stage(total[0], [total[k].astype(bf16) for k in range(1, p_n)], "p"))
    own_rows = jnp.concatenate(own, axis=1)

    y_near = lax.all_gather(own_rows.astype(bf16), ("p", "q"), axis=0, tiled=True)
    y_far = shift(y_near, "core", 1)

    gram = jnp.zeros((width // 2, width), f32)
    for rows_of in (y_near, y_far):
        mine = lax.dynamic_slice_in_dim(rows_of, ci * (width // 2), width // 2, axis=1)
        gram = gram + lax.dot_general(
            mine, rows_of, (((0,), (0,)), ((), ())), preferred_element_type=f32
        )
    gram = reduce_stage(gram, [gram] * (x_n - 1), "x") / all_rows
    gram = absolute([gram, shift(gram, "core", 1)], "core")
    lower = jnp.linalg.cholesky(gram)
    inverse = jax.scipy.linalg.solve_triangular(lower, jnp.eye(width, dtype=f32), lower=True)

    slots = x_n * q_n * p_n * cols_each
    kh = width // 2
    shapes = [
        jax.ShapeDtypeStruct((slots // x_n, wide, kh), f32 if k == 0 else bf16) for k in range(x_n)
    ] + [jax.ShapeDtypeStruct((slots // q_n, wide, kh), f32 if k == 0 else bf16) for k in range(q_n)]
    y_panels = (RB_DEV, wide, width)
    parts = block_products(
        functools.partial(project_kernel, len(sources), x_n, q_n),
        p_slot, p_panel, sources, y_near.reshape(y_panels), y_far.reshape(y_panels),
        min(2 * x_n * held, 2 * par * slot_cap * 2 * x_n), slots, shapes, "project_products",
    )
    by_x = reduce_stage(parts[0], parts[1:x_n], "x").reshape(q_n, p_n, cols_each * wide, kh)
    by_x = reduce_stage(by_x[0], [by_x[k].astype(bf16) for k in range(1, q_n)], "q")
    by_q = reduce_stage(parts[x_n], parts[x_n + 1 :], "q").reshape(x_n, p_n, cols_each * wide, kh)
    by_q = reduce_stage(by_q[0], [by_q[k].astype(bf16) for k in range(1, x_n)], "x")
    both = jnp.concatenate([by_x, by_q], axis=2)
    z_rows = reduce_stage(both[0], [both[k].astype(bf16) for k in range(1, p_n)], "p")

    basis = lax.dot_general(
        own_rows, inverse, (((1,), (1,)), ((), ())), precision=HIGHEST, preferred_element_type=f32
    ).astype(bf16)
    projected = lax.dot_general(
        inverse, z_rows, (((1,), (1,)), ((), ())), precision=HIGHEST, preferred_element_type=f32
    )
    projected = lax.all_to_all(projected, ("x", "core"), split_axis=0, concat_axis=1, tiled=True)
    return (basis, projected)


def solution(mesh):
    obs, par = mesh.shape["obs"], mesh.shape["par"]
    fine = Mesh(mesh.devices.reshape(obs // 2, 2, 4, par // 4), ALL)
    spread = P(ALL)
    placed = (
        P(ALL, None, None),
        P(ALL, None),
        spread,
        spread,
        P(("p", "q"), None),
    )
    return jax.shard_map(
        per_device,
        mesh=fine,
        in_specs=placed,
        out_specs=(P(ALL, None), P(("x", "core"), ("p", "q"))),
        check_vma=False,
    )
```

```python
import functools

import jax
import jax.numpy as jnp
from jax import lax
from jax.experimental import pallas as pl
from jax.experimental.pallas import tpu as pltpu
from jax.sharding import Mesh, PartitionSpec as P

RB_DEV = 32
UNROLL = 4
CHUNKS = 4
MOST_SLOTS = 512
VMEM_LIMIT = 60 * 1024 * 1024
HIGHEST = lax.Precision.HIGHEST
ALL = ("x", "core", "p", "q")


def shift(value, axis, by):
    size = lax.axis_size(axis)
    return lax.ppermute(value, axis, [(i, (i + by) % size) for i in range(size)])


def spread_pieces(value, axis):
    return [value] + [shift(value, axis, k) for k in range(1, lax.axis_size(axis))]


def reduce_stage(keep, sends, axis):
    total = keep
    for k, part in enumerate(sends, 1):
        total = total + shift(part, axis, k).astype(jnp.float32)
    return total


def passes_of(sources, bounds):
    groups, room = [], 0
    base = 0
    for source, bound in zip(sources, bounds):
        if not groups or room + bound > MOST_SLOTS:
            groups.append([])
            room = 0
        groups[-1].append((source, base))
        room += bound
        base += source.shape[0]
    return groups


def slots_of(bounds):
    most, room = 0, 0
    for bound in bounds:
        room = bound if room + bound > MOST_SLOTS else room + bound
        most = max(most, room)
    return most


def collect(rows_ref, cols_ref, group, slots, list_rows, list_cols, sem, spare):
    count = jnp.int32(0)
    for source, base in group:

        def take(i, count, source=source, base=base):
            row = rows_ref[base + i]

            @pl.when(row >= 0)
            def _():
                pltpu.make_async_copy(source.at[i], slots.at[count], sem).start()
                list_rows[count] = row
                list_cols[count] = cols_ref[base + i]

            return count + jnp.where(row >= 0, 1, 0).astype(jnp.int32)

        count = lax.fori_loop(0, source.shape[0], take, count)
    for extra in range(UNROLL - 1):
        list_rows[count + extra] = spare
        list_cols[count + extra] = 0

    def settle(i, carry):
        pltpu.make_async_copy(group[0][0].at[0], slots.at[0], sem).wait()
        return carry

    lax.fori_loop(0, count, settle, 0)
    return count


def accumulate(bounds, contract, rows_ref, cols_ref, sources, panel_copies, scratch):
    slots, panels, acc, list_rows, list_cols, sem, panel_sem = scratch
    copies = [
        pltpu.make_async_copy(source, target, panel_sem.at[i])
        for i, (source, target) in enumerate(panel_copies)
    ]
    for copy in copies:
        copy.start()
    spare = acc.shape[0] - 1

    def clear(i, carry):
        acc[i] = jnp.zeros(acc.shape[1:], acc.dtype)
        return carry

    lax.fori_loop(0, spare, clear, 0)

    def step(i, carry):
        for j in range(UNROLL):
            k = i * UNROLL + j
            row = list_rows[k]
            acc[row] += lax.dot_general(
                slots[k],
                panels[list_cols[k]],
                (((contract,), (0,)), ((), ())),
                preferred_element_type=jnp.float32,
            )
        return carry

    for turn, group in enumerate(passes_of(sources, bounds)):
        count = collect(rows_ref, cols_ref, group, slots, list_rows, list_cols, sem, spare)
        if turn == 0:
            for copy in copies:
                copy.wait()
        lax.fori_loop(0, (count + UNROLL - 1) // UNROLL, step, 0)


def sketch_kernel(bounds, pieces_n, rows_ref, cols_ref, *refs):
    n = len(bounds)
    sources, pieces = refs[:n], refs[n : n + pieces_n]
    outs, scratch = refs[n + pieces_n : -7], refs[-7:]
    panels, acc = scratch[1], scratch[2]
    each = pieces[0].shape[0]
    accumulate(
        bounds, 1, rows_ref, cols_ref, sources,
        [(piece, panels.at[pl.ds(i * each, each)]) for i, piece in enumerate(pieces)],
        scratch,
    )
    width = outs[0].shape[-1]
    chunks = acc.shape[-1] // width
    per = (acc.shape[0] - 1) // (len(outs) // chunks)
    for g in range(len(outs) // chunks):

        def give(i, carry, g=g):
            for c in range(chunks):
                out = outs[g * chunks + c]
                out[i] = acc[g * per + i, :, c * width : (c + 1) * width].astype(out.dtype)
            return carry

        lax.fori_loop(0, per, give, 0)


def project_kernel(bounds, pieces_n, x_n, q_n, rows_ref, cols_ref, *refs):
    n = len(bounds)
    sources, pieces = refs[:n], refs[n : n + pieces_n]
    outs, scratch = refs[n + pieces_n : -7], refs[-7:]
    panels, acc = scratch[1], scratch[2]
    parts = pieces_n // CHUNKS
    copies = []
    for c in range(CHUNKS):
        base = 0
        for piece in pieces[c * parts : (c + 1) * parts]:
            rows, cols = piece.shape[0], piece.shape[2]
            copies.append((piece, panels.at[pl.ds(base, rows), :, pl.ds(c * cols, cols)]))
            base += rows
    accumulate(bounds, 0, rows_ref, cols_ref, sources, copies, scratch)
    width = acc.shape[-1] // 2
    inner = (acc.shape[0] - 1) // (x_n * q_n)
    for g in range(x_n):

        def give_x(i, carry, g=g):
            out = outs[g]
            out[i] = acc[g * q_n * inner + i, :, :width].astype(out.dtype)
            return carry

        lax.fori_loop(0, q_n * inner, give_x, 0)
    for g in range(q_n):
        for x in range(x_n):

            def give_q(i, carry, g=g, x=x):
                out = outs[x_n + g]
                out[x * inner + i] = acc[(x * q_n + g) * inner + i, :, width:].astype(out.dtype)
                return carry

            lax.fori_loop(0, inner, give_q, 0)


def block_products(kernel, bounds, rows, cols, sources, pieces, panels_n, acc_n, width, outs, name):
    wide = sources[0].shape[1]
    smem = pl.BlockSpec(memory_space=pltpu.SMEM)
    anywhere = pl.BlockSpec(memory_space=pl.ANY)
    slots_n = slots_of(bounds)
    return pl.pallas_call(
        kernel,
        out_shape=outs,
        in_specs=[smem, smem] + [anywhere] * (len(sources) + len(pieces)),
        out_specs=[pl.BlockSpec(memory_space=pltpu.VMEM)] * len(outs),
        scratch_shapes=[
            pltpu.VMEM((slots_n + UNROLL, wide, wide), jnp.bfloat16),
            pltpu.VMEM((panels_n, wide, width), jnp.bfloat16),
            pltpu.VMEM((acc_n + 1, wide, width), jnp.float32),
            pltpu.SMEM((slots_n + UNROLL,), jnp.int32),
            pltpu.SMEM((slots_n + UNROLL,), jnp.int32),
            pltpu.SemaphoreType.DMA,
            pltpu.SemaphoreType.DMA((len(pieces),)),
        ],
        compiler_params=pltpu.CompilerParams(vmem_limit_bytes=VMEM_LIMIT),
        cost_estimate=pl.CostEstimate(
            flops=2 * 128 * wide * wide * width, bytes_accessed=32 << 20, transcendentals=0
        ),
        name=name,
    )(rows, cols, *sources, *pieces)


def dot32(a, b, dims):
    return lax.dot_general(
        a, b, (dims, ((), ())), precision=HIGHEST, preferred_element_type=jnp.float32
    )


def leaf_inverse(a):
    n = a.shape[0]
    place = lax.broadcasted_iota(jnp.int32, (n, 1), 0)
    rows = lax.broadcasted_iota(jnp.int32, (n, n), 0)
    cols = lax.broadcasted_iota(jnp.int32, (n, n), 1)
    both = jnp.concatenate([a, jnp.where(rows == cols, 1.0, 0.0).astype(a.dtype)], axis=1)
    pivots = jnp.ones((n, 1), a.dtype)
    for j in range(n):
        pivot = both[j : j + 1, j : j + 1]
        times = jnp.where(place > j, both[:, j : j + 1] * (1.0 / pivot), 0.0)
        pivots = jnp.where(place == j, pivot, pivots)
        both = both - times * both[j : j + 1, :]
    return both[:, n:] * lax.rsqrt(pivots)


def inverse_kernel(scale, k, *refs):
    gram, before, out = refs[: k + 1], refs[k + 1 : -1], refs[-1]
    n = out.shape[0]
    grams = [g[...] * scale for g in gram]
    rest = grams[k]
    factors = []
    for j in range(k):
        factor = dot32(grams[0], before[j][:, :n], ((1,), (1,)))
        for i in range(1, j + 1):
            factor += dot32(grams[i], before[j][:, i * n : (i + 1) * n], ((1,), (1,)))
        rest = rest - dot32(factor, factor, ((1,), (1,)))
        factors.append(factor)
    corner = leaf_inverse(rest)
    out[...] = jnp.zeros(out.shape, out.dtype)
    if k:
        total = dot32(factors[0], before[0][:, : k * n], ((1,), (0,)))
        for j in range(1, k):
            total += dot32(factors[j], before[j][:, : k * n], ((1,), (0,)))
        out[:, : k * n] = -dot32(corner, total, ((1,), (0,)))
    out[:, k * n : (k + 1) * n] = corner


def inverse_rows(scale, gram, before, width):
    k = len(before)
    n = gram[0].shape[0]
    return pl.pallas_call(
        functools.partial(inverse_kernel, scale, k),
        out_shape=jax.ShapeDtypeStruct((n, width), jnp.float32),
        compiler_params=pltpu.CompilerParams(vmem_limit_bytes=16 << 20),
        cost_estimate=pl.CostEstimate(flops=12 << 30, bytes_accessed=1 << 20, transcendentals=0),
        name="inverse_rows",
    )(*gram, *before)


def per_device(blocks, owner, row_local, col_local, sketch):
    x_n, q_n, p_n = lax.axis_size("x"), lax.axis_size("q"), lax.axis_size("p")
    xi, ci, zi, yi = (lax.axis_index(a) for a in ALL)
    par = p_n * q_n
    total_devs = 2 * x_n * par
    held, wide = blocks.shape[0], blocks.shape[1]
    width = sketch.shape[1]
    col_dev = sketch.shape[0] // wide
    slot_cap = max(2, (2 * held + total_devs - 1) // total_devs)
    rows_each = RB_DEV // par
    cols_each = col_dev // (2 * x_n)
    all_rows = RB_DEV * wide * 2 * x_n
    bf16, f32 = jnp.bfloat16, jnp.float32
    kc = width // CHUNKS
    by_q_n = held // 4
    by_x_n = held - by_q_n

    code = (owner[:, 0] * RB_DEV + row_local) * col_dev + col_local
    pair = jnp.concatenate([code, shift(code, "core", 1)])
    codes, sources = [pair], [blocks, shift(blocks, "core", 1)]
    first, last = blocks[:by_x_n], blocks[by_x_n:]
    most_y, most_p = min(by_x_n, par * slot_cap), min(by_x_n, 2 * par * slot_cap)
    bounds_y, bounds_p = [most_y + by_q_n] * 2, [most_p + by_q_n] * 2
    along_x = jnp.arange(held) < by_x_n
    along = [along_x, along_x]
    for k in range(1, x_n):
        got = shift(first, "x", k)
        sources += [got, shift(got, "core", 1)]
        bounds_y += [most_y] * 2
        bounds_p += [most_p] * 2
        there = shift(pair, "x", k).reshape(2, held)[:, :by_x_n]
        codes.append(there.reshape(-1))
        along.append(jnp.ones((2 * by_x_n,), bool))
    for k in range(1, q_n):
        got = shift(last, "q", k)
        sources += [got, shift(got, "core", 1)]
        bounds_y += [by_q_n] * 2
        bounds_p += [by_q_n] * 2
        there = shift(pair, "q", k).reshape(2, held)[:, by_x_n:]
        codes.append(there.reshape(-1))
        along.append(jnp.zeros((2 * by_q_n,), bool))
    codes, along = jnp.concatenate(codes), jnp.concatenate(along)

    half = col_dev // 2
    panels = sketch.reshape(col_dev, wide, width)
    mine = lax.dynamic_slice_in_dim(panels, ci * half, half, axis=0)
    near = []
    for part in (mine[: half // 2], mine[half // 2 :]):
        near += spread_pieces(jnp.concatenate(spread_pieces(part, "p")), "q")
    sketch_pieces = near + [shift(piece, "core", 1) for piece in near]

    owners = codes // (RB_DEV * col_dev)
    row = codes // col_dev % RB_DEV
    col = codes % col_dev
    o_obs, o_par = owners // par, owners % par
    o_x, o_core = o_obs // 2, o_obs % 2
    o_z, o_y = o_par // q_n, o_par % q_n
    r_par, r_in = row // rows_each, row % rows_each
    r_z, r_y = r_par // q_n, r_par % q_n
    c_x, c_core, c_in = col // (2 * cols_each), col // cols_each % 2, col % cols_each

    per = p_n * rows_each
    groups = q_n + x_n - 1
    other_x = q_n - 1 + (o_x - xi) % x_n
    y_group = jnp.where(along, (r_y - yi) % q_n, jnp.where(o_x == xi, 0, other_x))
    y_slot = (y_group * p_n + (r_z - zi) % p_n) * rows_each + r_in
    y_mine = (o_core == ci) & jnp.where(along, o_x == xi, r_y == yi)
    y_slot = jnp.where(y_mine, y_slot, -1)
    quarter = half // 2
    y_panel = jnp.where(col // half == ci, 0, 2) + col % half // quarter
    y_panel = (y_panel * q_n + (yi - o_y) % q_n) * p_n + (zi - o_z) % p_n
    y_panel = y_panel * quarter + col % quarter

    p_slot = ((c_x - xi) % x_n * q_n + (o_y - yi) % q_n) * p_n + (o_z - zi) % p_n
    p_slot = p_slot * cols_each + c_in
    p_mine = (c_core == ci) & jnp.where(along, o_x == xi, r_y == yi)
    p_slot = jnp.where(p_mine, p_slot, -1)
    in_part = (zi - r_z) % p_n * rows_each + r_in
    same_x = (jnp.where(o_core == ci, 0, q_n) + (yi - r_y) % q_n) * per
    not_x = (2 * q_n + jnp.where(o_core == ci, 0, x_n - 1) + (xi - o_x) % x_n - 1) * per
    p_panel = jnp.where(o_x == xi, same_x, not_x) + in_part

    shapes = []
    for g in range(groups):
        shapes += [jax.ShapeDtypeStruct((per, wide, kc), bf16 if g else f32)] * CHUNKS
    parts = block_products(
        functools.partial(sketch_kernel, bounds_y, len(sketch_pieces)), bounds_y,
        y_slot, y_panel, sources, sketch_pieces, par * col_dev, groups * per, width,
        shapes, "sketch_products",
    )
    own, y_pieces, inverse, gathered = [], [], [], []
    for c in range(CHUNKS):
        by_group = [parts[g * CHUNKS + c] for g in range(groups)]
        total = reduce_stage(by_group[0], by_group[1:q_n], "q")
        total = reduce_stage(total, by_group[q_n:], "x")
        total = total.reshape(p_n, rows_each * wide, kc)
        mine = reduce_stage(total[0], [total[k].astype(bf16) for k in range(1, p_n)], "p")
        own.append(mine)
        line = jnp.concatenate(spread_pieces(mine.astype(bf16), "p"))
        here = jnp.concatenate(spread_pieces(line, "q"))
        there = jnp.concatenate([shift(line, "x", k) for k in range(1, x_n)])
        here_far, there_far = shift(here, "core", 1), shift(there, "core", 1)
        y_pieces += [a.reshape(-1, wide, kc) for a in (here, here_far, there, there_far)]
        gathered.append((here, here_far))
        gram = []
        for before in gathered:
            gram.append(sum(
                lax.dot_general(a, b, (((0,), (0,)), ((), ())), preferred_element_type=f32)
                for a, b in zip(gathered[c], before)
            ))
        joined = jnp.concatenate(gram, axis=1)
        joined = reduce_stage(joined, [joined] * (x_n - 1), "x")
        gram = [joined[:, j * kc : (j + 1) * kc] for j in range(c + 1)]
        inverse.append(inverse_rows(1.0 / all_rows, gram, inverse, width))
    own_rows = jnp.concatenate(own, axis=1)

    slots = x_n * q_n * p_n * cols_each
    kh = width // 2
    shapes = [
        jax.ShapeDtypeStruct((slots // x_n, wide, kh), f32 if k == 0 else bf16) for k in range(x_n)
    ] + [jax.ShapeDtypeStruct((slots // q_n, wide, kh), f32 if k == 0 else bf16) for k in range(q_n)]
    parts = block_products(
        functools.partial(project_kernel, bounds_p, len(y_pieces), x_n, q_n), bounds_p,
        p_slot, p_panel, sources, y_pieces, 2 * groups * per, slots, width,
        shapes, "project_products",
    )
    by_x = reduce_stage(parts[0], parts[1:x_n], "x").reshape(q_n, p_n, cols_each * wide, kh)
    by_x = reduce_stage(by_x[0], [by_x[k].astype(bf16) for k in range(1, q_n)], "q")
    by_q = reduce_stage(parts[x_n], parts[x_n + 1 :], "q").reshape(x_n, p_n, cols_each * wide, kh)
    by_q = reduce_stage(by_q[0], [by_q[k].astype(bf16) for k in range(1, x_n)], "x")
    both = jnp.concatenate([by_x, by_q], axis=2)
    z_rows = reduce_stage(both[0], [both[k].astype(bf16) for k in range(1, p_n)], "p")

    inverse = jnp.concatenate(inverse, axis=0)
    basis = dot32(own_rows, inverse, ((1,), (1,))).astype(bf16)
    projected = dot32(inverse, z_rows, ((1,), (1,)))
    projected = lax.all_to_all(projected, ("x", "core"), split_axis=0, concat_axis=1, tiled=True)
    return (basis, projected)


def solution(mesh):
    obs, par = mesh.shape["obs"], mesh.shape["par"]
    fine = Mesh(mesh.devices.reshape(obs // 2, 2, 4, par // 4), ALL)
    spread = P(ALL)
    placed = (
        P(ALL, None, None),
        P(ALL, None),
        spread,
        spread,
        P(("p", "q"), None),
    )
    return jax.shard_map(
        per_device,
        mesh=fine,
        in_specs=placed,
        out_specs=(P(ALL, None), P(("x", "core"), ("p", "q"))),
        check_vma=False,
    )
```

```python
import functools

import jax
import jax.numpy as jnp
from jax import lax
from jax.experimental import pallas as pl
from jax.experimental.pallas import tpu as pltpu
from jax.sharding import Mesh, PartitionSpec as P

RB_DEV = 32
UNROLL = 4
CHUNKS = 2
LEAF = 128
MOST_SLOTS = 512
VMEM_LIMIT = 60 * 1024 * 1024
HIGHEST = lax.Precision.HIGHEST
ALL = ("x", "core", "p", "q")


def shift(value, axis, by):
    size = lax.axis_size(axis)
    return lax.ppermute(value, axis, [(i, (i + by) % size) for i in range(size)])


def swap(value, bit):
    size = lax.axis_size("p")
    return lax.ppermute(value, "p", [(i, i ^ bit) for i in range(size)])


def gather_p(value):
    pair = jnp.concatenate([value, swap(value, 2)])
    return jnp.concatenate([pair, swap(pair, 1)])


def reduce_p(total):
    part = total[:2] + swap(total[2:].astype(jnp.bfloat16), 1).astype(jnp.float32)
    return part[0] + swap(part[1].astype(jnp.bfloat16), 2).astype(jnp.float32)


def place_p(here, there):
    differs = here ^ there
    return (differs & 1) * 2 + (differs >> 1)


def together(*values):
    return lax.optimization_barrier(values)


def after(value, *others):
    return together(value, *others)[0]


def spread_pieces(value, axis):
    return [value] + [shift(value, axis, k) for k in range(1, lax.axis_size(axis))]


def reduce_stage(keep, sends, axis):
    total = keep
    for k, part in enumerate(sends, 1):
        total = total + shift(part, axis, k).astype(jnp.float32)
    return total


def passes_of(sources, bounds):
    groups, room = [], 0
    base = 0
    for source, bound in zip(sources, bounds):
        if not groups or room + bound > MOST_SLOTS:
            groups.append([])
            room = 0
        groups[-1].append((source, base))
        room += bound
        base += source.shape[0]
    return groups


def slots_of(bounds):
    most, room = 0, 0
    for bound in bounds:
        room = bound if room + bound > MOST_SLOTS else room + bound
        most = max(most, room)
    return most


def collect(rows_ref, cols_ref, group, slots, list_rows, list_cols, sem, spare):
    count = jnp.int32(0)
    for source, base in group:

        def take(i, count, source=source, base=base):
            row = rows_ref[base + i]

            @pl.when(row >= 0)
            def _():
                pltpu.make_async_copy(source.at[i], slots.at[count], sem).start()
                list_rows[count] = row
                list_cols[count] = cols_ref[base + i]

            return count + jnp.where(row >= 0, 1, 0).astype(jnp.int32)

        count = lax.fori_loop(0, source.shape[0], take, count)
    for extra in range(UNROLL - 1):
        list_rows[count + extra] = spare
        list_cols[count + extra] = 0

    def settle(i, carry):
        pltpu.make_async_copy(group[0][0].at[0], slots.at[0], sem).wait()
        return carry

    lax.fori_loop(0, count, settle, 0)
    return count


def accumulate(bounds, contract, rows_ref, cols_ref, sources, panel_copies, scratch):
    slots, panels, acc, list_rows, list_cols, sem, panel_sem = scratch
    copies = [
        pltpu.make_async_copy(source, target, panel_sem.at[i])
        for i, (source, target) in enumerate(panel_copies)
    ]
    for copy in copies:
        copy.start()
    spare = acc.shape[0] - 1

    def clear(i, carry):
        acc[i] = jnp.zeros(acc.shape[1:], acc.dtype)
        return carry

    lax.fori_loop(0, spare, clear, 0)

    def step(i, carry):
        for j in range(UNROLL):
            k = i * UNROLL + j
            row = list_rows[k]
            acc[row] += lax.dot_general(
                slots[k],
                panels[list_cols[k]],
                (((contract,), (0,)), ((), ())),
                preferred_element_type=jnp.float32,
            )
        return carry

    for turn, group in enumerate(passes_of(sources, bounds)):
        count = collect(rows_ref, cols_ref, group, slots, list_rows, list_cols, sem, spare)
        if turn == 0:
            for copy in copies:
                copy.wait()
        lax.fori_loop(0, (count + UNROLL - 1) // UNROLL, step, 0)


def sketch_kernel(bounds, pieces_n, rows_ref, cols_ref, *refs):
    n = len(bounds)
    sources, pieces = refs[:n], refs[n : n + pieces_n]
    outs, scratch = refs[n + pieces_n : -7], refs[-7:]
    panels, acc = scratch[1], scratch[2]
    each = pieces[0].shape[0]
    accumulate(
        bounds, 1, rows_ref, cols_ref, sources,
        [(piece, panels.at[pl.ds(i * each, each)]) for i, piece in enumerate(pieces)],
        scratch,
    )
    width = outs[0].shape[-1]
    chunks = acc.shape[-1] // width
    per = (acc.shape[0] - 1) // (len(outs) // chunks)
    for g in range(len(outs) // chunks):

        def give(i, carry, g=g):
            for c in range(chunks):
                out = outs[g * chunks + c]
                out[i] = acc[g * per + i, :, c * width : (c + 1) * width].astype(out.dtype)
            return carry

        lax.fori_loop(0, per, give, 0)


def project_kernel(bounds, pieces_n, x_n, q_n, rows_ref, cols_ref, *refs):
    n = len(bounds)
    sources, pieces = refs[:n], refs[n : n + pieces_n]
    outs, scratch = refs[n + pieces_n : -7], refs[-7:]
    panels, acc = scratch[1], scratch[2]
    parts = pieces_n // CHUNKS
    copies = []
    for c in range(CHUNKS):
        base = 0
        for piece in pieces[c * parts : (c + 1) * parts]:
            rows, cols = piece.shape[0], piece.shape[2]
            copies.append((piece, panels.at[pl.ds(base, rows), :, pl.ds(c * cols, cols)]))
            base += rows
    accumulate(bounds, 0, rows_ref, cols_ref, sources, copies, scratch)
    width = acc.shape[-1] // 2
    inner = (acc.shape[0] - 1) // (x_n * q_n)
    for g in range(x_n):

        def give_x(i, carry, g=g):
            out = outs[g]
            out[i] = acc[g * q_n * inner + i, :, :width].astype(out.dtype)
            return carry

        lax.fori_loop(0, q_n * inner, give_x, 0)
    for g in range(q_n):
        for x in range(x_n):

            def give_q(i, carry, g=g, x=x):
                out = outs[x_n + g]
                out[x * inner + i] = acc[(x * q_n + g) * inner + i, :, width:].astype(out.dtype)
                return carry

            lax.fori_loop(0, inner, give_q, 0)


def block_products(kernel, bounds, rows, cols, sources, pieces, panels_n, acc_n, width, outs, name):
    wide = sources[0].shape[1]
    smem = pl.BlockSpec(memory_space=pltpu.SMEM)
    anywhere = pl.BlockSpec(memory_space=pl.ANY)
    slots_n = slots_of(bounds)
    return pl.pallas_call(
        kernel,
        out_shape=outs,
        in_specs=[smem, smem] + [anywhere] * (len(sources) + len(pieces)),
        out_specs=[pl.BlockSpec(memory_space=pltpu.VMEM)] * len(outs),
        scratch_shapes=[
            pltpu.VMEM((slots_n + UNROLL, wide, wide), jnp.bfloat16),
            pltpu.VMEM((panels_n, wide, width), jnp.bfloat16),
            pltpu.VMEM((acc_n + 1, wide, width), jnp.float32),
            pltpu.SMEM((slots_n + UNROLL,), jnp.int32),
            pltpu.SMEM((slots_n + UNROLL,), jnp.int32),
            pltpu.SemaphoreType.DMA,
            pltpu.SemaphoreType.DMA((len(pieces),)),
        ],
        compiler_params=pltpu.CompilerParams(vmem_limit_bytes=VMEM_LIMIT),
        cost_estimate=pl.CostEstimate(
            flops=2 * 128 * wide * wide * width, bytes_accessed=32 << 20, transcendentals=0
        ),
        name=name,
    )(rows, cols, *sources, *pieces)


def dot32(a, b, dims):
    return lax.dot_general(
        a, b, (dims, ((), ())), precision=HIGHEST, preferred_element_type=jnp.float32
    )


def leaf_inverse(a):
    n = a.shape[0]
    place = lax.broadcasted_iota(jnp.int32, (n, 1), 0)
    rows = lax.broadcasted_iota(jnp.int32, (n, n), 0)
    cols = lax.broadcasted_iota(jnp.int32, (n, n), 1)
    both = jnp.concatenate([a, jnp.where(rows == cols, 1.0, 0.0).astype(a.dtype)], axis=1)
    pivots = jnp.ones((n, 1), a.dtype)
    for j in range(n):
        pivot = both[j : j + 1, j : j + 1]
        times = jnp.where(place > j, both[:, j : j + 1] * (1.0 / pivot), 0.0)
        pivots = jnp.where(place == j, pivot, pivots)
        both = both - times * both[j : j + 1, :]
    return both[:, n:] * lax.rsqrt(pivots)


def inverse_kernel(scale, k, first, gram, *refs):
    before, out = refs[:k], refs[-1]
    n = out.shape[0]
    grams = [gram[first : first + n, j * n : (j + 1) * n] * scale for j in range(k + 1)]
    rest = grams[k]
    factors = []
    for j in range(k):
        factor = dot32(grams[0], before[j][:, :n], ((1,), (1,)))
        for i in range(1, j + 1):
            factor += dot32(grams[i], before[j][:, i * n : (i + 1) * n], ((1,), (1,)))
        rest = rest - dot32(factor, factor, ((1,), (1,)))
        factors.append(factor)
    corner = leaf_inverse(rest)
    out[...] = jnp.zeros(out.shape, out.dtype)
    if k:
        total = dot32(factors[0], before[0][:, : k * n], ((1,), (0,)))
        for j in range(1, k):
            total += dot32(factors[j], before[j][:, : k * n], ((1,), (0,)))
        out[:, : k * n] = -dot32(corner, total, ((1,), (0,)))
    out[:, k * n : (k + 1) * n] = corner


def inverse_rows(scale, gram, first, before, width, late):
    vmem, anywhere = pl.BlockSpec(memory_space=pltpu.VMEM), pl.BlockSpec(memory_space=pl.ANY)
    return pl.pallas_call(
        functools.partial(inverse_kernel, scale, len(before), first),
        out_shape=jax.ShapeDtypeStruct((LEAF, width), jnp.float32),
        in_specs=[vmem] * (1 + len(before)) + [anywhere] * len(late),
        out_specs=vmem,
        compiler_params=pltpu.CompilerParams(vmem_limit_bytes=16 << 20),
        cost_estimate=pl.CostEstimate(flops=12 << 30, bytes_accessed=1 << 20, transcendentals=0),
        name="inverse_rows",
    )(gram, *before, *late)


def per_device(blocks, owner, row_local, col_local, sketch):
    x_n, q_n, p_n = lax.axis_size("x"), lax.axis_size("q"), lax.axis_size("p")
    xi, ci, zi, yi = (lax.axis_index(a) for a in ALL)
    par = p_n * q_n
    total_devs = 2 * x_n * par
    held, wide = blocks.shape[0], blocks.shape[1]
    width = sketch.shape[1]
    col_dev = sketch.shape[0] // wide
    slot_cap = max(2, (2 * held + total_devs - 1) // total_devs)
    rows_each = RB_DEV // par
    cols_each = col_dev // (2 * x_n)
    all_rows = RB_DEV * wide * 2 * x_n
    bf16, f32 = jnp.bfloat16, jnp.float32
    kc = width // CHUNKS
    by_q_n = held // 4
    by_x_n = held - by_q_n

    half = col_dev // 2
    quarter = half // 2
    panels = sketch.reshape(col_dev, wide, width)
    mine = lax.dynamic_slice_in_dim(panels, ci * half, half, axis=0)
    first, last = blocks[:by_x_n], blocks[by_x_n:]
    code = (owner[:, 0] * RB_DEV + row_local) * col_dev + col_local
    got_x = [shift(first, "x", k) for k in range(1, x_n)]
    got_q = [shift(last, "q", k) for k in range(1, q_n)]
    line = gather_p(mine[:quarter])
    line, got_q, sibling, code_far, mine = together(
        line, got_q, shift(blocks, "core", 1), shift(code, "core", 1), mine
    )
    pair = jnp.concatenate([code, code_far])
    code_x = [shift(pair, "x", k) for k in range(1, x_n)]
    code_q = [shift(pair, "q", k) for k in range(1, q_n)]
    early = spread_pieces(line, "q")
    line = gather_p(mine[quarter:])
    far_q = [shift(got, "core", 1) for got in got_q]
    line, early, far_q, code_q = together(line, early, far_q, code_q)
    later = spread_pieces(line, "q")
    early_far = [shift(piece, "core", 1) for piece in early]
    later, early_far, got_x, code_x = together(later, early_far, got_x, code_x)
    later_far = [shift(piece, "core", 1) for piece in later]
    far_x = [shift(got, "core", 1) for got in got_x]
    sketch_pieces = early + later + early_far + later_far

    sources, codes = [blocks, sibling], [pair]
    most_y, most_p = min(by_x_n, par * slot_cap), min(by_x_n, 2 * par * slot_cap)
    bounds_y, bounds_p = [most_y + by_q_n] * 2, [most_p + by_q_n] * 2
    along_x = jnp.arange(held) < by_x_n
    along = [along_x, along_x]
    for got, far, there in zip(got_x, far_x, code_x):
        sources += [got, far]
        bounds_y += [most_y] * 2
        bounds_p += [most_p] * 2
        codes.append(there.reshape(2, held)[:, :by_x_n].reshape(-1))
        along.append(jnp.ones((2 * by_x_n,), bool))
    for got, far, there in zip(got_q, far_q, code_q):
        sources += [got, far]
        bounds_y += [by_q_n] * 2
        bounds_p += [by_q_n] * 2
        codes.append(there.reshape(2, held)[:, by_x_n:].reshape(-1))
        along.append(jnp.zeros((2 * by_q_n,), bool))
    codes, along = jnp.concatenate(codes), jnp.concatenate(along)

    owners = codes // (RB_DEV * col_dev)
    row = codes // col_dev % RB_DEV
    col = codes % col_dev
    o_obs, o_par = owners // par, owners % par
    o_x, o_core = o_obs // 2, o_obs % 2
    o_z, o_y = o_par // q_n, o_par % q_n
    r_par, r_in = row // rows_each, row % rows_each
    r_z, r_y = r_par // q_n, r_par % q_n
    c_x, c_core, c_in = col // (2 * cols_each), col // cols_each % 2, col % cols_each

    per = p_n * rows_each
    groups = q_n + x_n - 1
    other_x = q_n - 1 + (o_x - xi) % x_n
    y_group = jnp.where(along, (r_y - yi) % q_n, jnp.where(o_x == xi, 0, other_x))
    y_slot = (y_group * p_n + place_p(zi, r_z)) * rows_each + r_in
    y_mine = (o_core == ci) & jnp.where(along, o_x == xi, r_y == yi)
    y_slot = jnp.where(y_mine, y_slot, -1)
    y_panel = jnp.where(col // half == ci, 0, 2) + col % half // quarter
    y_panel = (y_panel * q_n + (yi - o_y) % q_n) * p_n + place_p(zi, o_z)
    y_panel = y_panel * quarter + col % quarter

    p_slot = ((c_x - xi) % x_n * q_n + (o_y - yi) % q_n) * p_n + place_p(zi, o_z)
    p_slot = p_slot * cols_each + c_in
    p_mine = (c_core == ci) & jnp.where(along, o_x == xi, r_y == yi)
    p_slot = jnp.where(p_mine, p_slot, -1)
    in_part = place_p(zi, r_z) * rows_each + r_in
    same_x = (jnp.where(o_core == ci, 0, q_n) + (yi - r_y) % q_n) * per
    not_x = (2 * q_n + jnp.where(o_core == ci, 0, x_n - 1) + (xi - o_x) % x_n - 1) * per
    p_panel = jnp.where(o_x == xi, same_x, not_x) + in_part

    shapes = []
    for g in range(groups):
        shapes += [jax.ShapeDtypeStruct((per, wide, kc), bf16 if g else f32)] * CHUNKS
    parts = block_products(
        functools.partial(sketch_kernel, bounds_y, len(sketch_pieces)), bounds_y,
        y_slot, y_panel, sources, sketch_pieces, par * col_dev, groups * per, width,
        shapes, "sketch_products",
    )
    def received(c):
        by_group = [parts[g * CHUNKS + c] for g in range(groups)]
        return by_group[0], (
            [shift(by_group[k], "q", k) for k in range(1, q_n)]
            + [shift(by_group[q_n - 1 + k], "x", k) for k in range(1, x_n)]
        )

    def summed(keep, got):
        for part in got:
            keep = keep + part.astype(f32)
        return keep.reshape(p_n, rows_each * wide, kc)

    def spread(line):
        return (
            [shift(line, "q", k) for k in range(1, q_n)],
            [shift(line, "x", k) for k in range(1, x_n)],
        )

    def siblings(line, here, there):
        here, there = jnp.concatenate([line, *here]), jnp.concatenate(there)
        return here, there, shift(here, "core", 1), shift(there, "core", 1)

    keep_a, got_a = received(0)
    keep_b, got_b = received(1)
    got_a = together(*got_a)
    own_a = reduce_p(summed(keep_a, got_a))
    own_a, got_b = together(own_a, got_b)
    line_a = gather_p(own_a.astype(bf16))
    own_b = reduce_p(summed(keep_b, got_b))
    line_a, own_b = together(line_a, own_b)
    line_b = gather_p(own_b.astype(bf16))
    spread_a = spread(line_a)
    line_b, spread_a = together(line_b, spread_a)
    spread_b = spread(line_b)
    all_a = siblings(line_a, *spread_a)
    spread_b, all_a = together(spread_b, all_a)
    all_b = siblings(line_b, *spread_b)
    own, y_pieces, grams = [own_a, own_b], [], []
    for c, (here, there, here_far, there_far) in enumerate((all_a, all_b)):
        y_pieces += [a.reshape(-1, wide, kc) for a in (here, here_far, there, there_far)]
        gram = []
        for before in (all_a, all_b)[: c + 1]:
            gram.append(sum(
                lax.dot_general(a, b, (((0,), (0,)), ((), ())), preferred_element_type=f32)
                for a, b in ((here, before[0]), (here_far, before[2]))
            ))
        gram = jnp.concatenate(gram, axis=1)
        grams.append(reduce_stage(gram, [gram] * (x_n - 1), "x"))
    own_rows = jnp.concatenate(own, axis=1)

    inverse = []

    def more_rows(*late):
        k = len(inverse)
        gram = grams[k * LEAF // kc]
        inverse.append(
            inverse_rows(1.0 / all_rows, gram, k * LEAF % kc, inverse, width, late)
        )

    slots = x_n * q_n * p_n * cols_each
    kh = width // 2
    shapes = [
        jax.ShapeDtypeStruct((slots // x_n, wide, kh), f32 if k == 0 else bf16) for k in range(x_n)
    ] + [jax.ShapeDtypeStruct((slots // q_n, wide, kh), f32 if k == 0 else bf16) for k in range(q_n)]
    parts = block_products(
        functools.partial(project_kernel, bounds_p, len(y_pieces), x_n, q_n), bounds_p,
        p_slot, p_panel, sources, y_pieces, 2 * groups * per, slots, width,
        shapes, "project_products",
    )
    more_rows(parts[0])
    more_rows()
    by_x = reduce_stage(parts[0], parts[1:x_n], "x").reshape(q_n, p_n, cols_each * wide, kh)
    by_q = reduce_stage(parts[x_n], parts[x_n + 1 :], "q").reshape(x_n, p_n, cols_each * wide, kh)
    by_x, by_q = after((by_x, by_q), inverse[-1])
    by_x = reduce_stage(by_x[0], [by_x[k].astype(bf16) for k in range(1, q_n)], "q")
    by_q = reduce_stage(by_q[0], [by_q[k].astype(bf16) for k in range(1, x_n)], "x")
    more_rows()
    both = after(jnp.concatenate([by_x, by_q], axis=2), inverse[-1])
    z_rows = reduce_p(both)
    more_rows()

    inverse = jnp.concatenate(inverse, axis=0)
    basis = dot32(own_rows, inverse, ((1,), (1,))).astype(bf16)
    projected = dot32(inverse, z_rows, ((1,), (1,)))
    projected = lax.all_to_all(projected, ("x", "core"), split_axis=0, concat_axis=1, tiled=True)
    return (basis, projected)


def solution(mesh):
    obs, par = mesh.shape["obs"], mesh.shape["par"]
    fine = Mesh(mesh.devices.reshape(obs // 2, 2, 4, par // 4), ALL)
    spread = P(ALL)
    placed = (
        P(ALL, None, None),
        P(ALL, None),
        spread,
        spread,
        P(("p", "q"), None),
    )
    return jax.shard_map(
        per_device,
        mesh=fine,
        in_specs=placed,
        out_specs=(P(ALL, None), P(("x", "core"), ("p", "q"))),
        check_vma=False,
    )
```

```python
import functools

import jax
import jax.numpy as jnp
from jax import lax
from jax.experimental import pallas as pl
from jax.experimental.pallas import tpu as pltpu
from jax.sharding import Mesh, PartitionSpec as P

RB_DEV = 32
UNROLL = 32
AHEAD = 2
CHUNKS = 2
LEAF = 128
MOST_SLOTS = 512
VMEM_LIMIT = 60 * 1024 * 1024
HIGHEST = lax.Precision.HIGHEST
ALL = ("x", "core", "p", "q")


def shift(value, axis, by):
    size = lax.axis_size(axis)
    return lax.ppermute(value, axis, [(i, (i + by) % size) for i in range(size)])


def swap(value, bit):
    size = lax.axis_size("p")
    return lax.ppermute(value, "p", [(i, i ^ bit) for i in range(size)])


def gather_p(value):
    pair = jnp.concatenate([value, swap(value, 2)])
    return jnp.concatenate([pair, swap(pair, 1)])


def reduce_p(total):
    part = total[:2] + swap(total[2:].astype(jnp.bfloat16), 1).astype(jnp.float32)
    return part[0] + swap(part[1].astype(jnp.bfloat16), 2).astype(jnp.float32)


def place_p(here, there):
    differs = here ^ there
    return (differs & 1) * 2 + (differs >> 1)


def together(*values):
    return lax.optimization_barrier(values)


def after(value, *others):
    return together(value, *others)[0]


def spread_pieces(value, axis):
    return [value] + [shift(value, axis, k) for k in range(1, lax.axis_size(axis))]


def absolute(pieces, axis):
    size, me = len(pieces), lax.axis_index(axis)
    laid = jnp.concatenate(pieces + pieces[:-1], axis=0)
    rows = pieces[0].shape[0]
    return lax.dynamic_slice_in_dim(laid, (size - me) % size * rows, size * rows, axis=0)


def reduce_stage(keep, sends, axis):
    total = keep
    for k, part in enumerate(sends, 1):
        total = total + shift(part, axis, k).astype(jnp.float32)
    return total


def passes_of(bounds):
    groups, room = [], 0
    for i, bound in enumerate(bounds):
        if not groups or room + bound > MOST_SLOTS:
            groups.append([])
            room = 0
        groups[-1].append(i)
        room += bound
    return groups


def slots_of(bounds):
    return max(sum(bounds[i] for i in group) for group in passes_of(bounds))


def list_kernel(counts_in, bounds, spare, rows_ref, cols_ref, counts, index, rows, cols):
    base = [0]
    for held in counts_in:
        base.append(base[-1] + held)
    start = 0
    for group in passes_of(bounds):
        slot = jnp.int32(start)
        for s in group:

            def take(i, slot, s=s):
                row = rows_ref[base[s] + i]

                @pl.when(row >= 0)
                def _():
                    index[slot] = i
                    rows[slot] = row
                    cols[slot] = cols_ref[base[s] + i]

                return slot + jnp.where(row >= 0, 1, 0).astype(jnp.int32)

            before = slot
            slot = lax.fori_loop(0, counts_in[s], take, slot)
            counts[s] = slot - before
        for extra in range(UNROLL - 1):
            rows[slot + extra] = spare
            cols[slot + extra] = 0
        start += sum(bounds[s] for s in group) + UNROLL


def block_lists(counts_in, bounds, spare, rows, cols):
    smem = pl.BlockSpec(memory_space=pltpu.SMEM)
    size = sum(bounds) + UNROLL * len(passes_of(bounds))
    shape = jax.ShapeDtypeStruct((size,), jnp.int32)
    return pl.pallas_call(
        functools.partial(list_kernel, counts_in, bounds, spare),
        out_shape=[jax.ShapeDtypeStruct((len(bounds),), jnp.int32), shape, shape, shape],
        in_specs=[smem, smem],
        out_specs=[smem] * 4,
        cost_estimate=pl.CostEstimate(flops=4 << 30, bytes_accessed=1 << 14, transcendentals=0),
        name="block_lists",
    )(rows, cols)


def accumulate(bounds, contract, lists, sources, panel_copies, scratch):
    counts, index, list_rows, list_cols = lists
    slots, panels, acc, sem, panel_sem = scratch
    copies = [
        pltpu.make_async_copy(source, target, panel_sem.at[i])
        for i, (source, target) in enumerate(panel_copies)
    ]

    start = 0
    for turn, group in enumerate(passes_of(bounds)):
        count = jnp.int32(0)
        for s in group:

            def take(i, carry, s=s, count=count, start=start):
                slot = count + i
                pltpu.make_async_copy(
                    sources[s].at[index[start + slot]], slots.at[slot], sem
                ).start()
                return carry

            lax.fori_loop(0, counts[s], take, 0)
            count = count + counts[s]
        if turn == 0:
            for copy in copies:
                copy.start()

            def clear(i, carry):
                acc[i] = jnp.zeros(acc.shape[1:], acc.dtype)
                return carry

            lax.fori_loop(0, acc.shape[0] - 1, clear, 0)

        def settle(i, carry):
            pltpu.make_async_copy(sources[0].at[0], slots.at[0], sem).wait()
            return carry

        lax.fori_loop(0, count, settle, 0)
        if turn == 0:
            for copy in copies:
                copy.wait()

        def step(i, carry, start=start):
            for j in range(UNROLL):
                k = i * UNROLL + j
                row = list_rows[start + k]
                acc[row] += lax.dot_general(
                    slots[k],
                    panels[list_cols[start + k]],
                    (((contract,), (0,)), ((), ())),
                    preferred_element_type=jnp.float32,
                )
            return carry

        lax.fori_loop(0, (count + UNROLL - 1) // UNROLL, step, 0)
        start += sum(bounds[s] for s in group) + UNROLL


def sketch_kernel(bounds, pieces_n, chunk, *refs):
    n = len(bounds)
    lists, sources, pieces = refs[:4], refs[4 : 4 + n], refs[4 + n : 4 + n + pieces_n]
    outs, scratch = refs[4 + n + pieces_n : -5], refs[-5:]
    panels, acc = scratch[1], scratch[2]
    kc = acc.shape[-1]
    copies, base = [], 0
    for piece in pieces:
        rows = piece.shape[0]
        copies.append((piece.at[:, :, pl.ds(chunk * kc, kc)], panels.at[pl.ds(base, rows)]))
        base += rows
    accumulate(bounds, 1, lists, sources, copies, scratch)
    per = outs[0].shape[0]
    outs = outs[-((acc.shape[0] - 1) // per) :]
    for g, out in enumerate(outs):

        def give(i, carry, g=g, out=out):
            out[i] = acc[g * per + i].astype(out.dtype)
            return carry

        lax.fori_loop(0, per, give, 0)


def project_kernel(bounds, pieces_n, x_n, q_n, *refs):
    n = len(bounds)
    lists, sources, pieces = refs[:4], refs[4 : 4 + n], refs[4 + n : 4 + n + pieces_n]
    outs, scratch = refs[4 + n + pieces_n : -5], refs[-5:]
    panels, acc = scratch[1], scratch[2]
    copies, base = [], 0
    for piece in pieces:
        rows = piece.shape[0]
        copies.append((piece, panels.at[pl.ds(base, rows)]))
        base += rows
    accumulate(bounds, 0, lists, sources, copies, scratch)
    width = acc.shape[-1] // 2
    inner = (acc.shape[0] - 1) // (x_n * q_n)
    for g in range(x_n):

        def give_x(i, carry, g=g):
            out = outs[g]
            out[i] = acc[g * q_n * inner + i, :, :width].astype(out.dtype)
            return carry

        lax.fori_loop(0, q_n * inner, give_x, 0)
    for g in range(q_n):
        for x in range(x_n):

            def give_q(i, carry, g=g, x=x):
                out = outs[x_n + g]
                out[x * inner + i] = acc[(x * q_n + g) * inner + i, :, width:].astype(out.dtype)
                return carry

            lax.fori_loop(0, inner, give_q, 0)


def block_products(kernel, bounds, lists, sources, pieces, acc_n, width, outs, name, late=()):
    wide = sources[0].shape[1]
    smem = pl.BlockSpec(memory_space=pltpu.SMEM)
    anywhere = pl.BlockSpec(memory_space=pl.ANY)
    return pl.pallas_call(
        kernel,
        out_shape=outs,
        in_specs=[smem] * 4 + [anywhere] * (len(sources) + len(pieces) + len(late)),
        out_specs=[pl.BlockSpec(memory_space=pltpu.VMEM)] * len(outs),
        scratch_shapes=[
            pltpu.VMEM((slots_of(bounds) + UNROLL, wide, wide), jnp.bfloat16),
            pltpu.VMEM((sum(p.shape[0] for p in pieces), wide, width), jnp.bfloat16),
            pltpu.VMEM((acc_n + 1, wide, width), jnp.float32),
            pltpu.SemaphoreType.DMA,
            pltpu.SemaphoreType.DMA((len(pieces),)),
        ],
        compiler_params=pltpu.CompilerParams(vmem_limit_bytes=VMEM_LIMIT),
        cost_estimate=pl.CostEstimate(
            flops=2 * 128 * wide * wide * width, bytes_accessed=32 << 20, transcendentals=0
        ),
        name=name,
    )(*lists, *sources, *pieces, *late)


def dot32(a, b, dims):
    return lax.dot_general(
        a, b, (dims, ((), ())), precision=HIGHEST, preferred_element_type=jnp.float32
    )


def leaf_inverse(a):
    n = a.shape[0]
    place = lax.broadcasted_iota(jnp.int32, (n, n), 0)
    lane = lax.broadcasted_iota(jnp.int32, (n, n), 1)
    unit = jnp.where(place == lane, 1.0, 0.0).astype(a.dtype)
    pivots = jnp.ones((n, n), a.dtype)
    columns = {j: jnp.broadcast_to(a[:, j : j + 1], (n, n)) for j in range(AHEAD + 1)}
    for j in range(n):
        column = columns.pop(j)
        pivot = column[j : j + 1]
        times = jnp.where(place > j, column * (1.0 / pivot), 0.0)
        pivots = jnp.where(place == j, pivot, pivots)
        for t in columns:
            columns[t] = columns[t] - times * column[t : t + 1]
        a, unit = a - times * a[j : j + 1], unit - times * unit[j : j + 1]
        t = j + AHEAD + 1
        if t < n:
            columns[t] = jnp.broadcast_to(a[:, t : t + 1], (n, n))
    return unit * lax.rsqrt(pivots)


def inverse_kernel(scale, k, first, gram, *refs):
    before, out = refs[:k], refs[-1]
    n = out.shape[0]
    grams = [gram[first : first + n, j * n : (j + 1) * n] * scale for j in range(k + 1)]
    rest = grams[k]
    factors = []
    for j in range(k):
        factor = dot32(grams[0], before[j][:, :n], ((1,), (1,)))
        for i in range(1, j + 1):
            factor += dot32(grams[i], before[j][:, i * n : (i + 1) * n], ((1,), (1,)))
        rest = rest - dot32(factor, factor, ((1,), (1,)))
        factors.append(factor)
    corner = leaf_inverse(rest)
    out[...] = jnp.zeros(out.shape, out.dtype)
    if k:
        total = dot32(factors[0], before[0][:, : k * n], ((1,), (0,)))
        for j in range(1, k):
            total += dot32(factors[j], before[j][:, : k * n], ((1,), (0,)))
        out[:, : k * n] = -dot32(corner, total, ((1,), (0,)))
    out[:, k * n : (k + 1) * n] = corner


def inverse_rows(scale, gram, first, before, width, late):
    vmem, anywhere = pl.BlockSpec(memory_space=pltpu.VMEM), pl.BlockSpec(memory_space=pl.ANY)
    return pl.pallas_call(
        functools.partial(inverse_kernel, scale, len(before), first),
        out_shape=jax.ShapeDtypeStruct((LEAF, width), jnp.float32),
        in_specs=[vmem] * (1 + len(before)) + [anywhere] * len(late),
        out_specs=vmem,
        compiler_params=pltpu.CompilerParams(vmem_limit_bytes=16 << 20),
        cost_estimate=pl.CostEstimate(flops=6 << 30, bytes_accessed=1 << 20, transcendentals=0),
        name="inverse_rows",
    )(gram, *before, *late)


def per_device(blocks, owner, row_local, col_local, sketch):
    x_n, q_n, p_n = lax.axis_size("x"), lax.axis_size("q"), lax.axis_size("p")
    xi, ci, zi, yi = (lax.axis_index(a) for a in ALL)
    par = p_n * q_n
    total_devs = 2 * x_n * par
    held, wide = blocks.shape[0], blocks.shape[1]
    width = sketch.shape[1]
    col_dev = sketch.shape[0] // wide
    slot_cap = max(2, (2 * held + total_devs - 1) // total_devs)
    rows_each = RB_DEV // par
    cols_each = col_dev // (2 * x_n)
    all_rows = RB_DEV * wide * 2 * x_n
    bf16, f32 = jnp.bfloat16, jnp.float32
    kc = width // CHUNKS
    by_q_n = held // 4
    by_x_n = held - by_q_n

    by_x = [blocks[i * by_q_n : (i + 1) * by_q_n] for i in range(3)]
    last = blocks[by_x_n:]
    half = col_dev // 2
    early_n = half // 2
    later_n = half - early_n
    panels = sketch.reshape(col_dev, wide, width)
    mine = lax.dynamic_slice_in_dim(panels, ci * half, half, axis=0)
    code = (owner[:, 0] * RB_DEV + row_local) * col_dev + col_local

    def along_x(value):
        return [shift(value, "x", k) for k in range(1, x_n)]

    def along_q(value):
        return [shift(value, "q", k) for k in range(1, q_n)]

    def across(values):
        return [shift(value, "core", 1) for value in values]

    code_x, code_q, (code_far,) = along_x(code), along_q(code), across([code])
    by_x[0], code_x = together(by_x[0], code_x)
    last, code_q = together(last, code_q)
    line, got_0, got_q, (sibling,), code_far, mine, by_x = together(
        gather_p(mine[:early_n]), along_x(by_x[0]), along_q(last), across([blocks]),
        code_far, mine, by_x,
    )
    early = [line] + along_q(line)
    line, early, got_1, far_0, far_q, code_x_far, code_q_far, by_x = together(
        gather_p(mine[early_n:]), early, along_x(by_x[1]), across(got_0), across(got_q),
        across(code_x), across(code_q), by_x,
    )
    later = [line] + along_q(line)

    codes, along = [code, code_far], [jnp.arange(held) < by_x_n] * 2
    for i in range(3):
        for near, far in zip(code_x, code_x_far):
            codes += [c[i * by_q_n : (i + 1) * by_q_n] for c in (near, far)]
            along += [jnp.ones((by_q_n,), bool)] * 2
    for near, far in zip(code_q, code_q_far):
        codes += [near[by_x_n:], far[by_x_n:]]
        along += [jnp.zeros((by_q_n,), bool)] * 2
    counts = [c.shape[0] for c in codes]
    most_y, most_p = min(by_x_n, par * slot_cap), min(by_x_n, 2 * par * slot_cap)
    thirds = 6 * (x_n - 1)
    bounds_y = [most_y + by_q_n] * 2 + [min(by_q_n, most_y)] * thirds + [by_q_n] * (2 * q_n - 2)
    bounds_p = [most_p + by_q_n] * 2 + [min(by_q_n, most_p)] * thirds + [by_q_n] * (2 * q_n - 2)
    codes, along = jnp.concatenate(codes), jnp.concatenate(along)

    owners = codes // (RB_DEV * col_dev)
    row = codes // col_dev % RB_DEV
    col = codes % col_dev
    o_obs, o_par = owners // par, owners % par
    o_x, o_core = o_obs // 2, o_obs % 2
    o_z, o_y = o_par // q_n, o_par % q_n
    r_par, r_in = row // rows_each, row % rows_each
    r_z, r_y = r_par // q_n, r_par % q_n
    c_x, c_core, c_in = col // (2 * cols_each), col // cols_each % 2, col % cols_each

    per = p_n * rows_each
    groups = q_n + x_n - 1
    other_x = q_n - 1 + (o_x - xi) % x_n
    y_group = jnp.where(along, (r_y - yi) % q_n, jnp.where(o_x == xi, 0, other_x))
    y_slot = (y_group * p_n + place_p(zi, r_z)) * rows_each + r_in
    y_mine = (o_core == ci) & jnp.where(along, o_x == xi, r_y == yi)
    y_slot = jnp.where(y_mine, y_slot, -1)
    place = col % half
    device = (yi - o_y) % q_n * p_n + place_p(zi, o_z)
    y_panel = jnp.where(
        place < early_n,
        device * early_n + place,
        2 * par * early_n + device * later_n + place - early_n,
    )
    other = jnp.where(place < early_n, par * early_n, par * later_n)
    y_panel = y_panel + jnp.where(col // half == ci, 0, other)

    p_slot = ((c_x - xi) % x_n * q_n + (o_y - yi) % q_n) * p_n + place_p(zi, o_z)
    p_slot = p_slot * cols_each + c_in
    p_mine = (c_core == ci) & jnp.where(along, o_x == xi, r_y == yi)
    p_slot = jnp.where(p_mine, p_slot, -1)
    in_part = place_p(zi, r_z) * rows_each + r_in
    same_x = (jnp.where(o_core == ci, 0, q_n) + (yi - r_y) % q_n) * per
    not_x = (2 * q_n + jnp.where(o_core == ci, 0, x_n - 1) + (xi - o_x) % x_n - 1) * per
    p_panel = jnp.where(o_x == xi, same_x, not_x) + in_part

    slots = x_n * q_n * p_n * cols_each
    lists_y = block_lists(counts, bounds_y, groups * per, y_slot, y_panel)
    lists_p = block_lists(counts, bounds_p, slots, p_slot, p_panel)
    later, early_far, got_2, far_1, lists_y, lists_p = together(
        later, across(early), along_x(by_x[2]), across(got_1), lists_y, lists_p
    )
    later_far, far_2 = across(later), across(got_2)
    sketch_pieces = early + early_far + later + later_far
    sources = [blocks, sibling]
    for gots, fars in ((got_0, far_0), (got_1, far_1), (got_2, far_2), (got_q, far_q)):
        for got, far in zip(gots, fars):
            sources += [got, far]

    def y_products(chunk, late):
        shapes = [
            jax.ShapeDtypeStruct((per, wide, kc), bf16 if g else f32) for g in range(groups)
        ]
        return block_products(
            functools.partial(sketch_kernel, bounds_y, len(sketch_pieces), chunk), bounds_y,
            lists_y, sources, sketch_pieces, groups * per, kc, shapes, "sketch_products", late,
        )

    def y_received(parts):
        return (
            [shift(parts[k], "q", k) for k in range(1, q_n)]
            + [shift(parts[q_n - 1 + k], "x", k) for k in range(1, x_n)]
        )

    def y_summed(parts, got):
        keep = parts[0]
        for part in got:
            keep = keep + part.astype(f32)
        return reduce_p(keep.reshape(p_n, rows_each * wide, kc))

    def spread(line):
        return (
            [shift(line, "q", k) for k in range(1, q_n)],
            [shift(line, "x", k) for k in range(1, x_n)],
        )

    def siblings(line, here, there):
        here, there = jnp.concatenate([line, *here]), jnp.concatenate(there)
        return here, shift(here, "core", 1), there, shift(there, "core", 1)

    def gram_rows(parts, befores):
        return jnp.concatenate([
            sum(
                lax.dot_general(a, b, (((0,), (0,)), ((), ())), preferred_element_type=f32)
                for a, b in zip(parts[:2], before[:2])
            )
            for before in befores
        ], axis=1)

    def z_products(parts):
        kh = kc // 2
        shapes = [
            jax.ShapeDtypeStruct((slots // n, wide, kh), f32 if k == 0 else bf16)
            for n in (x_n, q_n) for k in range(n)
        ]
        pieces = [a.reshape(-1, wide, kc) for a in parts]
        return block_products(
            functools.partial(project_kernel, bounds_p, len(pieces), x_n, q_n), bounds_p,
            lists_p, sources, pieces, slots, kc, shapes, "project_products",
        )

    def z_first(parts):
        return (
            [shift(parts[k], "x", k) for k in range(1, x_n)],
            [shift(parts[x_n + k], "q", k) for k in range(1, q_n)],
        )

    def z_second(parts, got):
        by_x, by_q = parts[0], parts[x_n]
        for part in got[0]:
            by_x = by_x + part.astype(f32)
        for part in got[1]:
            by_q = by_q + part.astype(f32)
        by_x = by_x.reshape(q_n, p_n, cols_each * wide, kc // 2)
        by_q = by_q.reshape(x_n, p_n, cols_each * wide, kc // 2)
        by_x = reduce_stage(by_x[0], [by_x[k].astype(bf16) for k in range(1, q_n)], "q")
        by_q = reduce_stage(by_q[0], [by_q[k].astype(bf16) for k in range(1, x_n)], "x")
        return jnp.concatenate([by_x, by_q], axis=2)

    inverse = []

    def more_rows(gram, *late):
        inverse.append(
            inverse_rows(
                1.0 / all_rows, gram, len(inverse) * LEAF % kc, inverse, width, late
            )
        )
        return inverse[-1]

    parts_a = y_products(0, ())
    got_a = y_received(parts_a)
    got_a, parts_b = together(got_a, y_products(1, (parts_a[0],)))
    got_b = y_received(parts_b)
    own_a, got_b = together(y_summed(parts_a, got_a), got_b)
    line_a, own_b = together(gather_p(own_a.astype(bf16)), y_summed(parts_b, got_b))
    line_b, spread_a = together(gather_p(own_b.astype(bf16)), spread(line_a))
    spread_b = spread(line_b)
    all_a = together(siblings(line_a, *spread_a))[0]
    spread_b, zs_a, gram_a = together(spread_b, z_products(all_a), gram_rows(all_a, [all_a]))

    first_a = z_first(zs_a)
    got_gram = [shift(gram_a, "x", k) for k in range(1, x_n)]
    all_b = together(siblings(line_b, *spread_b))[0]
    first_a, zs_b = together(first_a, z_products(all_b))
    first_b = z_first(zs_b)
    gram_a = sum(after(got_gram, zs_b), gram_a)
    late_b = after(all_b, zs_b)
    mine_b = [lax.dynamic_slice_in_dim(part, ci * (kc // 2), kc // 2, axis=1) for part in late_b[:2]]
    gram_b = gram_rows(mine_b, [all_a, late_b])
    second_a = z_second(zs_a, first_a)
    more_rows(gram_a, zs_b[0])
    first_b, gram_b, _ = together(first_b, gram_b, inverse[-1])
    got_gram = [shift(gram_b, "x", k) for k in range(1, x_n)]
    second_b = z_second(zs_b, first_b)
    z_a = reduce_p(second_a)
    more_rows(gram_a, first_b[0][0])
    second_b, got_gram, _ = together(second_b, got_gram, inverse[-1])
    z_b = reduce_p(second_b)
    gram_b = sum(got_gram, gram_b)
    gram_b = absolute([gram_b, shift(gram_b, "core", 1)], "core")
    more_rows(gram_b)
    more_rows(gram_b)
    inverse = jnp.concatenate(inverse, axis=0)
    own_rows = jnp.concatenate([own_a, own_b], axis=1)
    basis = dot32(own_rows, inverse, ((1,), (1,))).astype(bf16)

    obs_n, me = 2 * x_n, xi * 2 + ci
    rows_n = width // obs_n
    turned = jnp.concatenate([inverse, inverse[:-rows_n]], axis=0)
    turned = lax.dynamic_slice_in_dim(turned, me * rows_n, width, axis=0)
    z_rows = jnp.concatenate([z_a, z_b], axis=1)
    kept, *sent = [
        dot32(turned[k * rows_n : (k + 1) * rows_n], z_rows, ((1,), (1,))) for k in range(obs_n)
    ]
    got = [
        lax.ppermute(part, ("x", "core"), [(i, (i + k) % obs_n) for i in range(obs_n)])
        for k, part in enumerate(sent, 1)
    ]
    laid = jnp.concatenate(got[::-1] + [kept] + got[::-1], axis=1)
    cols_n = kept.shape[1]
    projected = lax.dynamic_slice_in_dim(
        laid, (obs_n - 1 - me) * cols_n, obs_n * cols_n, axis=1
    )
    return (basis, projected)


def solution(mesh):
    obs, par = mesh.shape["obs"], mesh.shape["par"]
    fine = Mesh(mesh.devices.reshape(obs // 2, 2, 4, par // 4), ALL)
    spread = P(ALL)
    placed = (
        P(ALL, None, None),
        P(ALL, None),
        spread,
        spread,
        P(("p", "q"), None),
    )
    return jax.shard_map(
        per_device,
        mesh=fine,
        in_specs=placed,
        out_specs=(P(ALL, None), P(("x", "core"), ("p", "q"))),
        check_vma=False,
    )
```

```python
import functools

import jax
import jax.numpy as jnp
from jax import lax
from jax.experimental import pallas as pl
from jax.experimental.pallas import tpu as pltpu
from jax.sharding import Mesh, PartitionSpec as P

RB_DEV = 32
UNROLL = 32
AHEAD = 2
CHUNKS = 2
LEAF = 128
MOST_SLOTS = 512
VMEM_LIMIT = 60 * 1024 * 1024
HIGHEST = lax.Precision.HIGHEST
ALL = ("x", "core", "p", "q")


def shift(value, axis, by):
    size = lax.axis_size(axis)
    return lax.ppermute(value, axis, [(i, (i + by) % size) for i in range(size)])


def swap(value, bits):
    size = lax.axis_size("p")
    return lax.ppermute(value, "p", [(i, i ^ bits) for i in range(size)])


def place_p(here, there):
    differs = here ^ there
    return (differs & 1) * 2 + (differs >> 1)


def gather_p(value, direct=False):
    if direct:
        return jnp.concatenate([value] + [swap(value, bits) for bits in (2, 1, 3)])
    pair = jnp.concatenate([value, swap(value, 2)])
    return jnp.concatenate([pair, swap(pair, 1)])


def reduce_p(total, direct=False):
    f32, bf16 = jnp.float32, jnp.bfloat16
    if direct:
        got = [swap(total[i].astype(bf16), bits) for i, bits in ((1, 2), (2, 1), (3, 3))]
        return sum([part.astype(f32) for part in got], total[0])
    return reduce_rest(reduce_half(total))


def reduce_half(total):
    return total[:2] + swap(total[2:].astype(jnp.bfloat16), 1).astype(jnp.float32)


def reduce_rest(half):
    return half[0] + swap(half[1].astype(jnp.bfloat16), 2).astype(jnp.float32)


def together(*values):
    return lax.optimization_barrier(values)


def after(value, *others):
    return together(value, *others)[0]


def spread_pieces(value, axis):
    return [value] + [shift(value, axis, k) for k in range(1, lax.axis_size(axis))]


def absolute(pieces, axis):
    size, me = len(pieces), lax.axis_index(axis)
    laid = jnp.concatenate(pieces + pieces[:-1], axis=0)
    rows = pieces[0].shape[0]
    return lax.dynamic_slice_in_dim(laid, (size - me) % size * rows, size * rows, axis=0)


def reduce_stage(keep, sends, axis):
    total = keep
    for k, part in enumerate(sends, 1):
        total = total + shift(part, axis, k).astype(jnp.float32)
    return total


def passes_of(bounds):
    groups, room = [], 0
    for i, bound in enumerate(bounds):
        if not groups or room + bound > MOST_SLOTS:
            groups.append([])
            room = 0
        groups[-1].append(i)
        room += bound
    return groups


def slots_of(bounds):
    return max(sum(bounds[i] for i in group) for group in passes_of(bounds))


def list_kernel(counts_in, bounds, spare, rows_ref, cols_ref, counts, index, rows, cols):
    base = [0]
    for held in counts_in:
        base.append(base[-1] + held)
    start = 0
    for group in passes_of(bounds):
        slot = jnp.int32(start)
        for s in group:

            def take(i, slot, s=s):
                row = rows_ref[base[s] + i]

                @pl.when(row >= 0)
                def _():
                    index[slot] = i
                    rows[slot] = row
                    cols[slot] = cols_ref[base[s] + i]

                return slot + jnp.where(row >= 0, 1, 0).astype(jnp.int32)

            before = slot
            slot = lax.fori_loop(0, counts_in[s], take, slot)
            counts[s] = slot - before
        for extra in range(UNROLL - 1):
            rows[slot + extra] = spare
            cols[slot + extra] = 0
        start += sum(bounds[s] for s in group) + UNROLL


def block_lists(counts_in, bounds, spare, rows, cols):
    smem = pl.BlockSpec(memory_space=pltpu.SMEM)
    size = sum(bounds) + UNROLL * len(passes_of(bounds))
    shape = jax.ShapeDtypeStruct((size,), jnp.int32)
    return pl.pallas_call(
        functools.partial(list_kernel, counts_in, bounds, spare),
        out_shape=[jax.ShapeDtypeStruct((len(bounds),), jnp.int32), shape, shape, shape],
        in_specs=[smem, smem],
        out_specs=[smem] * 4,
        cost_estimate=pl.CostEstimate(flops=4 << 30, bytes_accessed=1 << 14, transcendentals=0),
        name="block_lists",
    )(rows, cols)


def accumulate(bounds, contract, lists, sources, panel_copies, scratch):
    counts, index, list_rows, list_cols = lists
    slots, panels, acc, sem, panel_sem = scratch
    copies = [
        pltpu.make_async_copy(source, target, panel_sem.at[i])
        for i, (source, target) in enumerate(panel_copies)
    ]

    start = 0
    for turn, group in enumerate(passes_of(bounds)):
        count = jnp.int32(0)
        for s in group:

            def take(i, carry, s=s, count=count, start=start):
                slot = count + i
                pltpu.make_async_copy(
                    sources[s].at[index[start + slot]], slots.at[slot], sem
                ).start()
                return carry

            lax.fori_loop(0, counts[s], take, 0)
            count = count + counts[s]
        if turn == 0:
            for copy in copies:
                copy.start()

            def clear(i, carry):
                acc[i] = jnp.zeros(acc.shape[1:], acc.dtype)
                return carry

            lax.fori_loop(0, acc.shape[0] - 1, clear, 0)

        def settle(i, carry):
            pltpu.make_async_copy(sources[0].at[0], slots.at[0], sem).wait()
            return carry

        lax.fori_loop(0, count, settle, 0)
        if turn == 0:
            for copy in copies:
                copy.wait()

        def step(i, carry, start=start):
            for j in range(UNROLL):
                k = i * UNROLL + j
                row = list_rows[start + k]
                acc[row] += lax.dot_general(
                    slots[k],
                    panels[list_cols[start + k]],
                    (((contract,), (0,)), ((), ())),
                    preferred_element_type=jnp.float32,
                )
            return carry

        lax.fori_loop(0, (count + UNROLL - 1) // UNROLL, step, 0)
        start += sum(bounds[s] for s in group) + UNROLL


def sketch_kernel(bounds, pieces_n, chunk, *refs):
    n = len(bounds)
    lists, sources, pieces = refs[:4], refs[4 : 4 + n], refs[4 + n : 4 + n + pieces_n]
    outs, scratch = refs[4 + n + pieces_n : -5], refs[-5:]
    panels, acc = scratch[1], scratch[2]
    kc = acc.shape[-1]
    copies, base = [], 0
    for piece in pieces:
        rows = piece.shape[0]
        copies.append((piece.at[:, :, pl.ds(chunk * kc, kc)], panels.at[pl.ds(base, rows)]))
        base += rows
    accumulate(bounds, 1, lists, sources, copies, scratch)
    per = outs[0].shape[0]
    outs = outs[-((acc.shape[0] - 1) // per) :]
    for g, out in enumerate(outs):

        def give(i, carry, g=g, out=out):
            out[i] = acc[g * per + i].astype(out.dtype)
            return carry

        lax.fori_loop(0, per, give, 0)


def project_kernel(bounds, pieces_n, x_n, q_n, *refs):
    n = len(bounds)
    lists, sources, pieces = refs[:4], refs[4 : 4 + n], refs[4 + n : 4 + n + pieces_n]
    outs, scratch = refs[4 + n + pieces_n : -5], refs[-5:]
    panels, acc = scratch[1], scratch[2]
    copies, base = [], 0
    for piece in pieces:
        rows = piece.shape[0]
        copies.append((piece, panels.at[pl.ds(base, rows)]))
        base += rows
    accumulate(bounds, 0, lists, sources, copies, scratch)
    width = acc.shape[-1] // 2
    inner = (acc.shape[0] - 1) // (x_n * q_n)
    for g in range(x_n):

        def give_x(i, carry, g=g):
            out = outs[g]
            out[i] = acc[g * q_n * inner + i, :, :width].astype(out.dtype)
            return carry

        lax.fori_loop(0, q_n * inner, give_x, 0)
    for g in range(q_n):
        for x in range(x_n):

            def give_q(i, carry, g=g, x=x):
                out = outs[x_n + g]
                out[x * inner + i] = acc[(x * q_n + g) * inner + i, :, width:].astype(out.dtype)
                return carry

            lax.fori_loop(0, inner, give_q, 0)


def block_products(kernel, bounds, lists, sources, pieces, acc_n, width, outs, name, late=()):
    wide = sources[0].shape[1]
    smem = pl.BlockSpec(memory_space=pltpu.SMEM)
    anywhere = pl.BlockSpec(memory_space=pl.ANY)
    return pl.pallas_call(
        kernel,
        out_shape=outs,
        in_specs=[smem] * 4 + [anywhere] * (len(sources) + len(pieces) + len(late)),
        out_specs=[pl.BlockSpec(memory_space=pltpu.VMEM)] * len(outs),
        scratch_shapes=[
            pltpu.VMEM((slots_of(bounds) + UNROLL, wide, wide), jnp.bfloat16),
            pltpu.VMEM((sum(p.shape[0] for p in pieces), wide, width), jnp.bfloat16),
            pltpu.VMEM((acc_n + 1, wide, width), jnp.float32),
            pltpu.SemaphoreType.DMA,
            pltpu.SemaphoreType.DMA((len(pieces),)),
        ],
        compiler_params=pltpu.CompilerParams(vmem_limit_bytes=VMEM_LIMIT),
        cost_estimate=pl.CostEstimate(
            flops=2 * 128 * wide * wide * width, bytes_accessed=32 << 20, transcendentals=0
        ),
        name=name,
    )(*lists, *sources, *pieces, *late)


def dot32(a, b, dims):
    return lax.dot_general(
        a, b, (dims, ((), ())), precision=HIGHEST, preferred_element_type=jnp.float32
    )


def leaf_inverse(a):
    n = a.shape[0]
    place = lax.broadcasted_iota(jnp.int32, (n, n), 0)
    lane = lax.broadcasted_iota(jnp.int32, (n, n), 1)
    unit = jnp.where(place == lane, 1.0, 0.0).astype(a.dtype)
    pivots = jnp.ones((n, n), a.dtype)
    columns = {j: jnp.broadcast_to(a[:, j : j + 1], (n, n)) for j in range(AHEAD + 1)}
    for j in range(n):
        column = columns.pop(j)
        pivot = column[j : j + 1]
        times = jnp.where(place > j, column * (1.0 / pivot), 0.0)
        pivots = jnp.where(place == j, pivot, pivots)
        for t in columns:
            columns[t] = columns[t] - times * column[t : t + 1]
        a, unit = a - times * a[j : j + 1], unit - times * unit[j : j + 1]
        t = j + AHEAD + 1
        if t < n:
            columns[t] = jnp.broadcast_to(a[:, t : t + 1], (n, n))
    return unit * lax.rsqrt(pivots)


def gram_kernel(n, core_ref, *refs):
    out = refs[-1]
    rows_n = out.shape[0]

    @pl.when(pl.program_id(0) == 0)
    def _():
        out[...] = jnp.zeros(out.shape, out.dtype)

    first_row = 0 if rows_n == refs[0].shape[1] else pl.multiple_of(core_ref[0] * rows_n, rows_n)
    some = pl.ds(first_row, rows_n)
    for first in range(0, len(refs) - 1, n):
        at = first // n * refs[0].shape[1]
        total = out[:, at : at + refs[0].shape[1]]
        for mine, other in zip(refs[-1 - n : -1], refs[first : first + n]):
            total += lax.dot_general(
                mine[:, some], other[...], (((0,), (0,)), ((), ())),
                preferred_element_type=jnp.float32,
            )
        out[:, at : at + refs[0].shape[1]] = total


def gram_rows(core, chunks, rows_n):
    n = len(chunks[-1])
    rows, cols = chunks[-1][0].shape
    steps = 4
    parts = [part for chunk in chunks for part in chunk]
    return pl.pallas_call(
        functools.partial(gram_kernel, n),
        grid=(steps,),
        out_shape=jax.ShapeDtypeStruct((rows_n, cols * len(chunks)), jnp.float32),
        in_specs=[pl.BlockSpec(memory_space=pltpu.SMEM)]
        + [pl.BlockSpec((rows // steps, cols), lambda i: (i, 0))] * len(parts),
        out_specs=pl.BlockSpec((rows_n, cols * len(chunks)), lambda i: (0, 0)),
        compiler_params=pltpu.CompilerParams(vmem_limit_bytes=24 << 20),
        cost_estimate=pl.CostEstimate(flops=2 << 30, bytes_accessed=8 << 20, transcendentals=0),
        name="gram_rows",
    )(core, *parts)


def inverse_kernel(scale, k, first, gram, *refs):
    before, out = refs[:k], refs[-1]
    n = out.shape[0]
    grams = [gram[first : first + n, j * n : (j + 1) * n] * scale for j in range(k + 1)]
    rest = grams[k]
    factors = []
    for j in range(k):
        factor = dot32(grams[0], before[j][:, :n], ((1,), (1,)))
        for i in range(1, j + 1):
            factor += dot32(grams[i], before[j][:, i * n : (i + 1) * n], ((1,), (1,)))
        rest = rest - dot32(factor, factor, ((1,), (1,)))
        factors.append(factor)
    corner = leaf_inverse(rest)
    out[...] = jnp.zeros(out.shape, out.dtype)
    if k:
        total = dot32(factors[0], before[0][:, : k * n], ((1,), (0,)))
        for j in range(1, k):
            total += dot32(factors[j], before[j][:, : k * n], ((1,), (0,)))
        out[:, : k * n] = -dot32(corner, total, ((1,), (0,)))
    out[:, k * n : (k + 1) * n] = corner


def inverse_rows(scale, gram, first, before, width, late):
    vmem, anywhere = pl.BlockSpec(memory_space=pltpu.VMEM), pl.BlockSpec(memory_space=pl.ANY)
    return pl.pallas_call(
        functools.partial(inverse_kernel, scale, len(before), first),
        out_shape=jax.ShapeDtypeStruct((LEAF, width), jnp.float32),
        in_specs=[vmem] * (1 + len(before)) + [anywhere] * len(late),
        out_specs=vmem,
        compiler_params=pltpu.CompilerParams(vmem_limit_bytes=16 << 20),
        cost_estimate=pl.CostEstimate(flops=1 << 26, bytes_accessed=1 << 16, transcendentals=0),
        name="inverse_rows",
    )(gram, *before, *late)


def per_device(blocks, owner, row_local, col_local, sketch):
    x_n, q_n, p_n = lax.axis_size("x"), lax.axis_size("q"), lax.axis_size("p")
    xi, ci, zi, yi = (lax.axis_index(a) for a in ALL)
    par = p_n * q_n
    total_devs = 2 * x_n * par
    held, wide = blocks.shape[0], blocks.shape[1]
    width = sketch.shape[1]
    col_dev = sketch.shape[0] // wide
    slot_cap = max(2, (2 * held + total_devs - 1) // total_devs)
    rows_each = RB_DEV // par
    cols_each = col_dev // (2 * x_n)
    all_rows = RB_DEV * wide * 2 * x_n
    bf16, f32 = jnp.bfloat16, jnp.float32
    kc = width // CHUNKS
    by_q_n = held // 4
    by_x_n = held - by_q_n

    first, last = blocks[:by_q_n], blocks[by_x_n:]
    half = col_dev // 2
    early_n = half // 2
    later_n = half - early_n
    panels = sketch.reshape(col_dev, wide, width)
    mine = lax.dynamic_slice_in_dim(panels, ci * half, half, axis=0)
    code = (owner[:, 0] * RB_DEV + row_local) * col_dev + col_local

    def along_x(value):
        return [shift(value, "x", k) for k in range(1, x_n)]

    def along_q(value):
        return [shift(value, "q", k) for k in range(1, q_n)]

    def across(values):
        return [shift(value, "core", 1) for value in values]

    code_x, code_q, (code_far,) = along_x(code), along_q(code), across([code])
    first, code_x = together(first, code_x)
    last, code_q = together(last, code_q)
    line, got_0, got_q, (sibling,), code_far, mine, second = together(
        gather_p(mine[:early_n]), along_x(first), along_q(last), across([blocks]),
        code_far, mine, after(blocks, code_far)[by_q_n : 2 * by_q_n],
    )
    third = after(blocks, second)[2 * by_q_n : by_x_n]
    early = [line] + along_q(line)
    line, early, got_1, far_0, far_q, code_x_far, code_q_far, third = together(
        gather_p(mine[early_n:]), early, along_x(second), across(got_0), across(got_q),
        across(code_x), across(code_q), third,
    )
    later = [line] + along_q(line)

    codes, along = [code, code_far], [jnp.arange(held) < by_x_n] * 2
    for i in range(3):
        for near, far in zip(code_x, code_x_far):
            codes += [c[i * by_q_n : (i + 1) * by_q_n] for c in (near, far)]
            along += [jnp.ones((by_q_n,), bool)] * 2
    for near, far in zip(code_q, code_q_far):
        codes += [near[by_x_n:], far[by_x_n:]]
        along += [jnp.zeros((by_q_n,), bool)] * 2
    counts = [c.shape[0] for c in codes]
    most_y, most_p = min(by_x_n, par * slot_cap), min(by_x_n, 2 * par * slot_cap)
    thirds = 6 * (x_n - 1)
    bounds_y = [most_y + by_q_n] * 2 + [min(by_q_n, most_y)] * thirds + [by_q_n] * (2 * q_n - 2)
    bounds_p = [most_p + by_q_n] * 2 + [min(by_q_n, most_p)] * thirds + [by_q_n] * (2 * q_n - 2)
    codes, along = jnp.concatenate(codes), jnp.concatenate(along)

    owners = codes // (RB_DEV * col_dev)
    row = codes // col_dev % RB_DEV
    col = codes % col_dev
    o_obs, o_par = owners // par, owners % par
    o_x, o_core = o_obs // 2, o_obs % 2
    o_z, o_y = o_par // q_n, o_par % q_n
    r_par, r_in = row // rows_each, row % rows_each
    r_z, r_y = r_par // q_n, r_par % q_n
    c_x, c_core, c_in = col // (2 * cols_each), col // cols_each % 2, col % cols_each

    per = p_n * rows_each
    groups = q_n + x_n - 1
    other_x = q_n - 1 + (o_x - xi) % x_n
    y_group = jnp.where(along, (r_y - yi) % q_n, jnp.where(o_x == xi, 0, other_x))
    y_slot = (y_group * p_n + place_p(zi, r_z)) * rows_each + r_in
    y_mine = (o_core == ci) & jnp.where(along, o_x == xi, r_y == yi)
    y_slot = jnp.where(y_mine, y_slot, -1)
    place = col % half
    device = (yi - o_y) % q_n * p_n + place_p(zi, o_z)
    y_panel = jnp.where(
        place < early_n,
        device * early_n + place,
        2 * par * early_n + device * later_n + place - early_n,
    )
    other = jnp.where(place < early_n, par * early_n, par * later_n)
    y_panel = y_panel + jnp.where(col // half == ci, 0, other)

    p_slot = ((c_x - xi) % x_n * q_n + (o_y - yi) % q_n) * p_n + place_p(zi, o_z)
    p_slot = p_slot * cols_each + c_in
    p_mine = (c_core == ci) & jnp.where(along, o_x == xi, r_y == yi)
    p_slot = jnp.where(p_mine, p_slot, -1)
    in_part = place_p(zi, r_z) * rows_each + r_in
    y_part = jnp.where(o_x == xi, (yi - r_y) % q_n, q_n - 1 + (xi - o_x) % x_n)
    p_panel = (jnp.where(o_core == ci, 0, groups) + y_part) * per + in_part
    slots = x_n * q_n * p_n * cols_each
    lists_y = block_lists(counts, bounds_y, groups * per, y_slot, y_panel)
    lists_p = block_lists(counts, bounds_p, slots, p_slot, p_panel)
    later, early_far, got_2, far_1, lists_y, lists_p = together(
        later, across(early), along_x(third), across(got_1), lists_y, lists_p
    )
    later_far, far_2 = across(later), across(got_2)
    sketch_pieces = early + early_far + later + later_far
    sources = [blocks, sibling]
    for gots, fars in ((got_0, far_0), (got_1, far_1), (got_2, far_2), (got_q, far_q)):
        for got, far in zip(gots, fars):
            sources += [got, far]

    def y_products(chunk, late):
        shapes = [
            jax.ShapeDtypeStruct((per, wide, kc), bf16 if g else f32) for g in range(groups)
        ]
        return block_products(
            functools.partial(sketch_kernel, bounds_y, len(sketch_pieces), chunk), bounds_y,
            lists_y, sources, sketch_pieces, groups * per, kc, shapes, "sketch_products", late,
        )

    def y_received(parts):
        return (
            [shift(parts[k], "q", k) for k in range(1, q_n)]
            + [shift(parts[q_n - 1 + k], "x", k) for k in range(1, x_n)]
        )

    def y_summed(parts, got, direct):
        keep = parts[0]
        for part in got:
            keep = keep + part.astype(f32)
        return reduce_p(keep.reshape(p_n, rows_each * wide, kc), direct)

    def spread(line):
        return (
            [shift(line, "q", k) for k in range(1, q_n)],
            [shift(line, "x", k) for k in range(1, x_n)],
        )

    def same_x(parts):
        return parts[:q_n] + parts[groups : groups + q_n]

    def z_products(parts):
        kh = kc // 2
        shapes = [
            jax.ShapeDtypeStruct((slots // n, wide, kh), f32 if k == 0 else bf16)
            for n in (x_n, q_n) for k in range(n)
        ]
        pieces = [a.reshape(-1, wide, kc) for a in parts]
        return block_products(
            functools.partial(project_kernel, bounds_p, len(pieces), x_n, q_n), bounds_p,
            lists_p, sources, pieces, slots, kc, shapes, "project_products",
        )

    def z_first(parts):
        return (
            [shift(parts[k], "x", k) for k in range(1, x_n)],
            [shift(parts[x_n + k], "q", k) for k in range(1, q_n)],
        )

    def z_summed(parts, got):
        by_x, by_q = parts[0], parts[x_n]
        for part in got[0]:
            by_x = by_x + part.astype(f32)
        for part in got[1]:
            by_q = by_q + part.astype(f32)
        return (
            by_x.reshape(q_n, p_n, cols_each * wide, kc // 2),
            by_q.reshape(x_n, p_n, cols_each * wide, kc // 2),
        )

    def z_second(by_x, by_q):
        by_x = reduce_stage(by_x[0], [by_x[k].astype(bf16) for k in range(1, q_n)], "q")
        by_q = reduce_stage(by_q[0], [by_q[k].astype(bf16) for k in range(1, x_n)], "x")
        return jnp.concatenate([by_x, by_q], axis=2)

    inverse = []

    def more_rows(gram, *late):
        inverse.append(
            inverse_rows(
                1.0 / all_rows, gram, len(inverse) * LEAF % kc, inverse, width, late
            )
        )
        return inverse[-1]

    core = jnp.reshape(ci, (1,)).astype(jnp.int32)
    parts_a = y_products(0, ())
    got_a = y_received(parts_a)
    got_a, parts_b = together(got_a, y_products(1, (parts_a[0],)))
    got_b = y_received(parts_b)
    own_a, got_b = together(y_summed(parts_a, got_a, True), got_b)
    line_a, own_b = together(gather_p(own_a.astype(bf16)), y_summed(parts_b, got_b, False))
    line_b, spread_a = together(gather_p(own_b.astype(bf16), True), spread(line_a))
    spread_b = spread(line_b)
    all_a = [line_a, *spread_a[0], *spread_a[1]]
    all_a = together(all_a + across(all_a))[0]
    near_a = same_x(all_a)
    line_b_far, spread_b, zs_a, gram_a = together(
        across([line_b]), spread_b, z_products(all_a), gram_rows(core, [near_a], kc)
    )

    first_a = z_first(zs_a)
    got_gram = along_x(gram_a)
    spread_b = spread_b[0] + spread_b[1]
    all_b = together([line_b, *spread_b, *line_b_far, *across(spread_b)])[0]
    first_a, zs_b = together(first_a, z_products(all_b))
    first_b = z_first(zs_b)
    second_a = z_second(*z_summed(zs_a, first_a))
    gram_a = sum(after(got_gram, zs_b), gram_a)
    more_rows(gram_a, zs_b[0])
    gram_b = gram_rows(core, [near_a, same_x(after(all_b, zs_b))], kc // 2)
    first_b, gram_b, _ = together(first_b, gram_b, inverse[-1])
    got_gram = along_x(gram_b)
    summed_b = z_summed(zs_b, first_b)
    second_b = z_second(*summed_b)
    z_a = reduce_p(after(second_a, summed_b))
    more_rows(gram_a, summed_b[0])
    second_b, _ = together(second_b, inverse[-1])
    half_b = reduce_half(second_b)
    gram_b = sum(got_gram, gram_b)
    gram_b = absolute([gram_b, shift(gram_b, "core", 1)], "core")
    more_rows(gram_b)
    half_b, _ = together(half_b, inverse[-1])
    z_b = reduce_rest(half_b)
    more_rows(gram_b, half_b)
    inverse = jnp.concatenate(inverse, axis=0)
    own_rows = jnp.concatenate([own_a, own_b], axis=1)

    obs_n, me = 2 * x_n, xi * 2 + ci
    rows_n = width // obs_n
    turned = jnp.concatenate([inverse, inverse[:-rows_n]], axis=0)
    turned = lax.dynamic_slice_in_dim(turned, me * rows_n, width, axis=0)
    z_rows = jnp.concatenate([z_a, z_b], axis=1)
    kept, *sent = [
        dot32(turned[k * rows_n : (k + 1) * rows_n], z_rows, ((1,), (1,))) for k in range(obs_n)
    ]
    basis = dot32(after(own_rows, sent), inverse, ((1,), (1,))).astype(bf16)
    got = [
        lax.ppermute(part, ("x", "core"), [(i, (i + k) % obs_n) for i in range(obs_n)])
        for k, part in enumerate(sent, 1)
    ]
    laid = jnp.concatenate(got[::-1] + [kept] + got[::-1], axis=1)
    cols_n = kept.shape[1]
    projected = lax.dynamic_slice_in_dim(
        laid, (obs_n - 1 - me) * cols_n, obs_n * cols_n, axis=1
    )
    return (basis, projected)


def solution(mesh):
    obs, par = mesh.shape["obs"], mesh.shape["par"]
    fine = Mesh(mesh.devices.reshape(obs // 2, 2, 4, par // 4), ALL)
    spread = P(ALL)
    placed = (
        P(ALL, None, None),
        P(ALL, None),
        spread,
        spread,
        P(("p", "q"), None),
    )
    return jax.shard_map(
        per_device,
        mesh=fine,
        in_specs=placed,
        out_specs=(P(ALL, None), P(("x", "core"), ("p", "q"))),
        check_vma=False,
    )
```

```python
import functools

import jax
import jax.numpy as jnp
from jax import lax
from jax.experimental import pallas as pl
from jax.experimental.pallas import tpu as pltpu
from jax.sharding import Mesh, PartitionSpec as P

RB_DEV = 32
UNROLL = 32
AHEAD = 2
WAITS = 16
CHUNKS = 2
LEAF = 128
MOST_SLOTS = 512
VMEM_LIMIT = 60 * 1024 * 1024
HIGHEST = lax.Precision.HIGHEST
ALL = ("x", "core", "p", "q")


def shift(value, axis, by):
    size = lax.axis_size(axis)
    return lax.ppermute(value, axis, [(i, (i + by) % size) for i in range(size)])


def swap(value, bits):
    size = lax.axis_size("p")
    return lax.ppermute(value, "p", [(i, i ^ bits) for i in range(size)])


def place_p(here, there):
    differs = here ^ there
    return (differs & 1) * 2 + (differs >> 1)


def gather_p(value, direct=False):
    if direct:
        return jnp.concatenate([value] + [swap(value, bits) for bits in (2, 1, 3)])
    pair = jnp.concatenate([value, swap(value, 2)])
    return jnp.concatenate([pair, swap(pair, 1)])


def reduce_p(total, direct=False):
    f32, bf16 = jnp.float32, jnp.bfloat16
    if direct:
        got = [swap(total[i].astype(bf16), bits) for i, bits in ((1, 2), (2, 1), (3, 3))]
        return sum([part.astype(f32) for part in got], total[0])
    return reduce_rest(reduce_half(total))


def reduce_half(total):
    return total[:2] + swap(total[2:].astype(jnp.bfloat16), 1).astype(jnp.float32)


def reduce_rest(half):
    return half[0] + swap(half[1].astype(jnp.bfloat16), 2).astype(jnp.float32)


def together(*values):
    return lax.optimization_barrier(values)


def after(value, *others):
    return together(value, *others)[0]


def spread_pieces(value, axis):
    return [value] + [shift(value, axis, k) for k in range(1, lax.axis_size(axis))]


def absolute(pieces, axis):
    size, me = len(pieces), lax.axis_index(axis)
    laid = jnp.concatenate(pieces + pieces[:-1], axis=0)
    rows = pieces[0].shape[0]
    return lax.dynamic_slice_in_dim(laid, (size - me) % size * rows, size * rows, axis=0)


def reduce_stage(keep, sends, axis):
    total = keep
    for k, part in enumerate(sends, 1):
        total = total + shift(part, axis, k).astype(jnp.float32)
    return total


def passes_of(bounds):
    groups, room = [], 0
    for i, bound in enumerate(bounds):
        if not groups or room + bound > MOST_SLOTS:
            groups.append([])
            room = 0
        groups[-1].append(i)
        room += bound
    return groups


def slots_of(bounds):
    return max(sum(bounds[i] for i in group) for group in passes_of(bounds))


def list_kernel(counts_in, bounds, spare, rows_ref, cols_ref, counts, index, rows, cols):
    base = [0]
    for held in counts_in:
        base.append(base[-1] + held)
    start = 0
    for group in passes_of(bounds):
        slot = jnp.int32(start)
        for s in group:

            def take(i, slot, s=s):
                row = rows_ref[base[s] + i]

                @pl.when(row >= 0)
                def _():
                    index[slot] = i
                    rows[slot] = row
                    cols[slot] = cols_ref[base[s] + i]

                return slot + jnp.where(row >= 0, 1, 0).astype(jnp.int32)

            before = slot
            slot = lax.fori_loop(0, counts_in[s], take, slot)
            counts[s] = slot - before
        for extra in range(UNROLL - 1):
            rows[slot + extra] = spare
            cols[slot + extra] = 0
        start += sum(bounds[s] for s in group) + UNROLL


def block_lists(counts_in, bounds, spare, rows, cols):
    smem = pl.BlockSpec(memory_space=pltpu.SMEM)
    size = sum(bounds) + UNROLL * len(passes_of(bounds))
    shape = jax.ShapeDtypeStruct((size,), jnp.int32)
    return pl.pallas_call(
        functools.partial(list_kernel, counts_in, bounds, spare),
        out_shape=[jax.ShapeDtypeStruct((len(bounds),), jnp.int32), shape, shape, shape],
        in_specs=[smem, smem],
        out_specs=[smem] * 4,
        cost_estimate=pl.CostEstimate(flops=4 << 30, bytes_accessed=1 << 14, transcendentals=0),
        name="block_lists",
    )(rows, cols)


def accumulate(bounds, contract, lists, sources, panel_copies, scratch):
    counts, index, list_rows, list_cols = lists
    slots, panels, acc, sem, panel_sem = scratch
    copies = [
        pltpu.make_async_copy(source, target, panel_sem.at[i])
        for i, (source, target) in enumerate(panel_copies)
    ]
    for copy in copies:
        copy.start()

    start = 0
    for turn, group in enumerate(passes_of(bounds)):
        count = jnp.int32(0)
        for s in group:

            def take(i, carry, s=s, count=count, start=start):
                slot = count + i
                pltpu.make_async_copy(
                    sources[s].at[index[start + slot]], slots.at[slot], sem
                ).start()
                return carry

            lax.fori_loop(0, counts[s], take, 0)
            count = count + counts[s]
        if turn == 0:

            def clear(i, carry):
                acc[i] = jnp.zeros(acc.shape[1:], acc.dtype)
                return carry

            lax.fori_loop(0, acc.shape[0] - 1, clear, 0)

        def settle(i, carry, n=1):
            some = pl.ds(0, n)
            pltpu.make_async_copy(sources[0].at[some], slots.at[some], sem).wait()
            return carry

        lax.fori_loop(0, count // WAITS, functools.partial(settle, n=WAITS), 0)
        lax.fori_loop(0, count % WAITS, settle, 0)
        if turn == 0:
            for copy in copies:
                copy.wait()

        def step(i, carry, start=start):
            for j in range(UNROLL):
                k = i * UNROLL + j
                row = list_rows[start + k]
                acc[row] += lax.dot_general(
                    slots[k],
                    panels[list_cols[start + k]],
                    (((contract,), (0,)), ((), ())),
                    preferred_element_type=jnp.float32,
                )
            return carry

        lax.fori_loop(0, (count + UNROLL - 1) // UNROLL, step, 0)
        start += sum(bounds[s] for s in group) + UNROLL


def sketch_kernel(bounds, pieces_n, chunk, *refs):
    n = len(bounds)
    lists, sources, pieces = refs[:4], refs[4 : 4 + n], refs[4 + n : 4 + n + pieces_n]
    outs, scratch = refs[4 + n + pieces_n : -5], refs[-5:]
    panels, acc = scratch[1], scratch[2]
    kc = acc.shape[-1]
    copies, base = [], 0
    for piece in pieces:
        rows = piece.shape[0]
        copies.append((piece.at[:, :, pl.ds(chunk * kc, kc)], panels.at[pl.ds(base, rows)]))
        base += rows
    accumulate(bounds, 1, lists, sources, copies, scratch)
    per = outs[0].shape[0]
    outs = outs[-((acc.shape[0] - 1) // per) :]
    for g, out in enumerate(outs):

        def give(i, carry, g=g, out=out):
            out[i] = acc[g * per + i].astype(out.dtype)
            return carry

        lax.fori_loop(0, per, give, 0)


def project_kernel(bounds, pieces_n, x_n, q_n, *refs):
    n = len(bounds)
    lists, sources, pieces = refs[:4], refs[4 : 4 + n], refs[4 + n : 4 + n + pieces_n]
    outs, scratch = refs[4 + n + pieces_n : -5], refs[-5:]
    panels, acc = scratch[1], scratch[2]
    copies, base = [], 0
    for piece in pieces:
        rows = piece.shape[0]
        copies.append((piece, panels.at[pl.ds(base, rows)]))
        base += rows
    accumulate(bounds, 0, lists, sources, copies, scratch)
    width = acc.shape[-1] // 2
    inner = (acc.shape[0] - 1) // (x_n * q_n)
    for g in range(x_n):

        def give_x(i, carry, g=g):
            out = outs[g]
            out[i] = acc[g * q_n * inner + i, :, :width].astype(out.dtype)
            return carry

        lax.fori_loop(0, q_n * inner, give_x, 0)
    for g in range(q_n):
        for x in range(x_n):

            def give_q(i, carry, g=g, x=x):
                out = outs[x_n + g]
                out[x * inner + i] = acc[(x * q_n + g) * inner + i, :, width:].astype(out.dtype)
                return carry

            lax.fori_loop(0, inner, give_q, 0)


def block_products(kernel, bounds, lists, sources, pieces, acc_n, width, outs, name, late=()):
    wide = sources[0].shape[1]
    smem = pl.BlockSpec(memory_space=pltpu.SMEM)
    anywhere = pl.BlockSpec(memory_space=pl.ANY)
    return pl.pallas_call(
        kernel,
        out_shape=outs,
        in_specs=[smem] * 4 + [anywhere] * (len(sources) + len(pieces) + len(late)),
        out_specs=[pl.BlockSpec(memory_space=pltpu.VMEM)] * len(outs),
        scratch_shapes=[
            pltpu.VMEM((slots_of(bounds) + UNROLL, wide, wide), jnp.bfloat16),
            pltpu.VMEM((sum(p.shape[0] for p in pieces), wide, width), jnp.bfloat16),
            pltpu.VMEM((acc_n + 1, wide, width), jnp.float32),
            pltpu.SemaphoreType.DMA,
            pltpu.SemaphoreType.DMA((len(pieces),)),
        ],
        compiler_params=pltpu.CompilerParams(vmem_limit_bytes=VMEM_LIMIT),
        cost_estimate=pl.CostEstimate(
            flops=2 * 128 * wide * wide * width, bytes_accessed=32 << 20, transcendentals=0
        ),
        name=name,
    )(*lists, *sources, *pieces, *late)


def dot32(a, b, dims):
    return lax.dot_general(
        a, b, (dims, ((), ())), precision=HIGHEST, preferred_element_type=jnp.float32
    )


def leaf_inverse(a):
    n = a.shape[0]
    place = lax.broadcasted_iota(jnp.int32, (n, n), 0)
    lane = lax.broadcasted_iota(jnp.int32, (n, n), 1)
    unit = jnp.where(place == lane, 1.0, 0.0).astype(a.dtype)
    pivots = jnp.ones((n, n), a.dtype)
    columns = {j: jnp.broadcast_to(a[:, j : j + 1], (n, n)) for j in range(AHEAD + 1)}
    for j in range(n):
        column = columns.pop(j)
        pivot = column[j : j + 1]
        times = jnp.where(place > j, column * (1.0 / pivot), 0.0)
        pivots = jnp.where(place == j, pivot, pivots)
        for t in columns:
            columns[t] = columns[t] - times * column[t : t + 1]
        a, unit = a - times * a[j : j + 1], unit - times * unit[j : j + 1]
        t = j + AHEAD + 1
        if t < n:
            columns[t] = jnp.broadcast_to(a[:, t : t + 1], (n, n))
    return unit * lax.rsqrt(pivots)


def gram_kernel(n, core_ref, *refs):
    out = refs[-1]
    rows_n = out.shape[0]

    @pl.when(pl.program_id(0) == 0)
    def _():
        out[...] = jnp.zeros(out.shape, out.dtype)

    first_row = 0 if rows_n == refs[0].shape[1] else pl.multiple_of(core_ref[0] * rows_n, rows_n)
    some = pl.ds(first_row, rows_n)
    for first in range(0, len(refs) - 1, n):
        at = first // n * refs[0].shape[1]
        total = out[:, at : at + refs[0].shape[1]]
        for mine, other in zip(refs[-1 - n : -1], refs[first : first + n]):
            total += lax.dot_general(
                mine[:, some], other[...], (((0,), (0,)), ((), ())),
                preferred_element_type=jnp.float32,
            )
        out[:, at : at + refs[0].shape[1]] = total


def gram_rows(core, chunks, rows_n):
    n = len(chunks[-1])
    rows, cols = chunks[-1][0].shape
    steps = 4
    parts = [part for chunk in chunks for part in chunk]
    return pl.pallas_call(
        functools.partial(gram_kernel, n),
        grid=(steps,),
        out_shape=jax.ShapeDtypeStruct((rows_n, cols * len(chunks)), jnp.float32),
        in_specs=[pl.BlockSpec(memory_space=pltpu.SMEM)]
        + [pl.BlockSpec((rows // steps, cols), lambda i: (i, 0))] * len(parts),
        out_specs=pl.BlockSpec((rows_n, cols * len(chunks)), lambda i: (0, 0)),
        compiler_params=pltpu.CompilerParams(vmem_limit_bytes=24 << 20),
        cost_estimate=pl.CostEstimate(flops=2 << 30, bytes_accessed=8 << 20, transcendentals=0),
        name="gram_rows",
    )(core, *parts)


def inverse_kernel(scale, k, first, gram, *refs):
    before, out = refs[:k], refs[-1]
    n = out.shape[0]
    grams = [gram[first : first + n, j * n : (j + 1) * n] * scale for j in range(k + 1)]
    rest = grams[k]
    factors = []
    for j in range(k):
        factor = dot32(grams[0], before[j][:, :n], ((1,), (1,)))
        for i in range(1, j + 1):
            factor += dot32(grams[i], before[j][:, i * n : (i + 1) * n], ((1,), (1,)))
        rest = rest - dot32(factor, factor, ((1,), (1,)))
        factors.append(factor)
    corner = leaf_inverse(rest)
    out[...] = jnp.zeros(out.shape, out.dtype)
    if k:
        total = dot32(factors[0], before[0][:, : k * n], ((1,), (0,)))
        for j in range(1, k):
            total += dot32(factors[j], before[j][:, : k * n], ((1,), (0,)))
        out[:, : k * n] = -dot32(corner, total, ((1,), (0,)))
    out[:, k * n : (k + 1) * n] = corner


def inverse_rows(scale, gram, first, before, width, late):
    vmem, anywhere = pl.BlockSpec(memory_space=pltpu.VMEM), pl.BlockSpec(memory_space=pl.ANY)
    return pl.pallas_call(
        functools.partial(inverse_kernel, scale, len(before), first),
        out_shape=jax.ShapeDtypeStruct((LEAF, width), jnp.float32),
        in_specs=[vmem] * (1 + len(before)) + [anywhere] * len(late),
        out_specs=vmem,
        compiler_params=pltpu.CompilerParams(vmem_limit_bytes=16 << 20),
        cost_estimate=pl.CostEstimate(flops=1 << 26, bytes_accessed=1 << 16, transcendentals=0),
        name="inverse_rows",
    )(gram, *before, *late)


def per_device(blocks, owner, row_local, col_local, sketch):
    x_n, q_n, p_n = lax.axis_size("x"), lax.axis_size("q"), lax.axis_size("p")
    xi, ci, zi, yi = (lax.axis_index(a) for a in ALL)
    par = p_n * q_n
    total_devs = 2 * x_n * par
    held, wide = blocks.shape[0], blocks.shape[1]
    width = sketch.shape[1]
    col_dev = sketch.shape[0] // wide
    slot_cap = max(2, (2 * held + total_devs - 1) // total_devs)
    rows_each = RB_DEV // par
    cols_each = col_dev // (2 * x_n)
    all_rows = RB_DEV * wide * 2 * x_n
    bf16, f32 = jnp.bfloat16, jnp.float32
    kc = width // CHUNKS
    by_q_n = held // 4
    by_x_n = held - by_q_n

    first, last = blocks[:by_q_n], blocks[by_x_n:]
    half = col_dev // 2
    early_n = half // 2
    later_n = half - early_n
    panels = sketch.reshape(col_dev, wide, width)
    mine = lax.dynamic_slice_in_dim(panels, ci * half, half, axis=0)
    code = (owner[:, 0] * RB_DEV + row_local) * col_dev + col_local

    def along_x(value):
        return [shift(value, "x", k) for k in range(1, x_n)]

    def along_q(value):
        return [shift(value, "q", k) for k in range(1, q_n)]

    def across(values):
        return [shift(value, "core", 1) for value in values]

    code_x, code_q, (code_far,) = along_x(code), along_q(code), across([code])
    first, code_x = together(first, code_x)
    last, code_q = together(last, code_q)
    line, got_0, got_q, (sibling,), code_far, mine, second = together(
        gather_p(mine[:early_n]), along_x(first), along_q(last), across([blocks]),
        code_far, mine, after(blocks, code_far)[by_q_n : 2 * by_q_n],
    )
    third = after(blocks, second)[2 * by_q_n : by_x_n]
    early = [line] + along_q(line)
    line, early, got_1, far_0, far_q, code_x_far, code_q_far, third = together(
        gather_p(mine[early_n:]), early, along_x(second), across(got_0), across(got_q),
        across(code_x), across(code_q), third,
    )
    later = [line] + along_q(line)

    codes, along = [code, code_far], [jnp.arange(held) < by_x_n] * 2
    for i in range(3):
        for near, far in zip(code_x, code_x_far):
            codes += [c[i * by_q_n : (i + 1) * by_q_n] for c in (near, far)]
            along += [jnp.ones((by_q_n,), bool)] * 2
    for near, far in zip(code_q, code_q_far):
        codes += [near[by_x_n:], far[by_x_n:]]
        along += [jnp.zeros((by_q_n,), bool)] * 2
    counts = [c.shape[0] for c in codes]
    most_y, most_p = min(by_x_n, par * slot_cap), min(by_x_n, 2 * par * slot_cap)
    thirds = 6 * (x_n - 1)
    bounds_y = [most_y + by_q_n] * 2 + [min(by_q_n, most_y)] * thirds + [by_q_n] * (2 * q_n - 2)
    bounds_p = [most_p + by_q_n] * 2 + [min(by_q_n, most_p)] * thirds + [by_q_n] * (2 * q_n - 2)
    codes, along = jnp.concatenate(codes), jnp.concatenate(along)

    owners = codes // (RB_DEV * col_dev)
    row = codes // col_dev % RB_DEV
    col = codes % col_dev
    o_obs, o_par = owners // par, owners % par
    o_x, o_core = o_obs // 2, o_obs % 2
    o_z, o_y = o_par // q_n, o_par % q_n
    r_par, r_in = row // rows_each, row % rows_each
    r_z, r_y = r_par // q_n, r_par % q_n
    c_x, c_core, c_in = col // (2 * cols_each), col // cols_each % 2, col % cols_each

    per = p_n * rows_each
    groups = q_n + x_n - 1
    other_x = q_n - 1 + (o_x - xi) % x_n
    y_group = jnp.where(along, (r_y - yi) % q_n, jnp.where(o_x == xi, 0, other_x))
    y_slot = (y_group * p_n + place_p(zi, r_z)) * rows_each + r_in
    y_mine = (o_core == ci) & jnp.where(along, o_x == xi, r_y == yi)
    y_slot = jnp.where(y_mine, y_slot, -1)
    place = col % half
    device = (yi - o_y) % q_n * p_n + place_p(zi, o_z)
    y_panel = jnp.where(
        place < early_n,
        device * early_n + place,
        2 * par * early_n + device * later_n + place - early_n,
    )
    other = jnp.where(place < early_n, par * early_n, par * later_n)
    y_panel = y_panel + jnp.where(col // half == ci, 0, other)

    p_slot = ((c_x - xi) % x_n * q_n + (o_y - yi) % q_n) * p_n + place_p(zi, o_z)
    p_slot = p_slot * cols_each + c_in
    p_mine = (c_core == ci) & jnp.where(along, o_x == xi, r_y == yi)
    p_slot = jnp.where(p_mine, p_slot, -1)
    in_part = place_p(zi, r_z) * rows_each + r_in
    y_part = jnp.where(o_x == xi, (yi - r_y) % q_n, q_n - 1 + (xi - o_x) % x_n)
    p_panel = (jnp.where(o_core == ci, 0, groups) + y_part) * per + in_part
    slots = x_n * q_n * p_n * cols_each
    lists_y = block_lists(counts, bounds_y, groups * per, y_slot, y_panel)
    lists_p = block_lists(counts, bounds_p, slots, p_slot, p_panel)
    later, early_far, got_2, far_1, lists_y, lists_p = together(
        later, across(early), along_x(third), across(got_1), lists_y, lists_p
    )
    later_far, far_2 = across(later), across(got_2)
    sketch_pieces = early + early_far + later + later_far
    sources = [blocks, sibling]
    for gots, fars in ((got_0, far_0), (got_1, far_1), (got_2, far_2), (got_q, far_q)):
        for got, far in zip(gots, fars):
            sources += [got, far]

    def y_products(chunk, late):
        shapes = [
            jax.ShapeDtypeStruct((per, wide, kc), bf16 if g else f32) for g in range(groups)
        ]
        return block_products(
            functools.partial(sketch_kernel, bounds_y, len(sketch_pieces), chunk), bounds_y,
            lists_y, sources, sketch_pieces, groups * per, kc, shapes, "sketch_products", late,
        )

    def y_received(parts):
        return (
            [shift(parts[k], "q", k) for k in range(1, q_n)]
            + [shift(parts[q_n - 1 + k], "x", k) for k in range(1, x_n)]
        )

    def y_summed(parts, got, direct):
        keep = parts[0]
        for part in got:
            keep = keep + part.astype(f32)
        return reduce_p(keep.reshape(p_n, rows_each * wide, kc), direct)

    def spread(line):
        return (
            [shift(line, "q", k) for k in range(1, q_n)],
            [shift(line, "x", k) for k in range(1, x_n)],
        )

    def same_x(parts):
        return parts[:q_n] + parts[groups : groups + q_n]

    def z_products(parts):
        kh = kc // 2
        shapes = [
            jax.ShapeDtypeStruct((slots // n, wide, kh), f32 if k == 0 else bf16)
            for n in (x_n, q_n) for k in range(n)
        ]
        pieces = [a.reshape(-1, wide, kc) for a in parts]
        return block_products(
            functools.partial(project_kernel, bounds_p, len(pieces), x_n, q_n), bounds_p,
            lists_p, sources, pieces, slots, kc, shapes, "project_products",
        )

    def z_first(parts):
        return (
            [shift(parts[k], "x", k) for k in range(1, x_n)],
            [shift(parts[x_n + k], "q", k) for k in range(1, q_n)],
        )

    def z_summed(parts, got):
        by_x, by_q = parts[0], parts[x_n]
        for part in got[0]:
            by_x = by_x + part.astype(f32)
        for part in got[1]:
            by_q = by_q + part.astype(f32)
        return (
            by_x.reshape(q_n, p_n, cols_each * wide, kc // 2),
            by_q.reshape(x_n, p_n, cols_each * wide, kc // 2),
        )

    def z_second(by_x, by_q):
        by_x = reduce_stage(by_x[0], [by_x[k].astype(bf16) for k in range(1, q_n)], "q")
        by_q = reduce_stage(by_q[0], [by_q[k].astype(bf16) for k in range(1, x_n)], "x")
        return jnp.concatenate([by_x, by_q], axis=2)

    inverse = []

    def more_rows(gram, *late):
        inverse.append(
            inverse_rows(
                1.0 / all_rows, gram, len(inverse) * LEAF % kc, inverse, width, late
            )
        )
        return inverse[-1]

    core = jnp.reshape(ci, (1,)).astype(jnp.int32)
    parts_a = y_products(0, ())
    got_a = y_received(parts_a)
    got_a, parts_b = together(got_a, y_products(1, (parts_a[0],)))
    got_b = y_received(parts_b)
    own_a, got_b = together(y_summed(parts_a, got_a, True), got_b)
    line_a, own_b = together(gather_p(own_a.astype(bf16)), y_summed(parts_b, got_b, False))
    line_b, spread_a = together(gather_p(own_b.astype(bf16), True), spread(line_a))
    spread_b = spread(line_b)
    all_a = [line_a, *spread_a[0], *spread_a[1]]
    all_a = together(all_a + across(all_a))[0]
    near_a = same_x(all_a)
    line_b_far, spread_b, zs_a, gram_a = together(
        across([line_b]), spread_b, z_products(all_a), gram_rows(core, [near_a], kc)
    )

    first_a = z_first(zs_a)
    got_gram = along_x(gram_a)
    spread_b = spread_b[0] + spread_b[1]
    all_b = together([line_b, *spread_b, *line_b_far, *across(spread_b)])[0]
    gram_b = gram_rows(core, [near_a, same_x(all_b)], kc // 2)
    got_b = along_x(gram_b)
    first_a, zs_b, got_b = together(first_a, z_products(after(all_b, gram_b)), got_b)
    first_b = z_first(zs_b)
    gram_b = sum(got_b, gram_b)
    gram_b = absolute([gram_b, shift(gram_b, "core", 1)], "core")
    gram_a = sum(after(got_gram, zs_b), gram_a)
    second_a = z_second(*z_summed(zs_a, first_a))
    more_rows(gram_a, zs_b[0])
    more_rows(gram_a)
    first_b, gram_b, _ = together(first_b, gram_b, inverse[-1])
    summed_b = z_summed(zs_b, first_b)
    second_b = z_second(*summed_b)
    z_a = reduce_p(after(second_a, summed_b))
    more_rows(gram_b, summed_b[0])
    second_b, _ = together(second_b, inverse[-1])
    half_b = reduce_half(second_b)
    more_rows(gram_b, second_b)
    half_b, _ = together(half_b, inverse[-1])
    z_b = reduce_rest(half_b)
    inverse = jnp.concatenate(inverse, axis=0)
    own_rows = jnp.concatenate([own_a, own_b], axis=1)

    obs_n, me = 2 * x_n, xi * 2 + ci
    rows_n = width // obs_n
    turned = jnp.concatenate([inverse, inverse[:-rows_n]], axis=0)
    turned = lax.dynamic_slice_in_dim(turned, me * rows_n, width, axis=0)
    z_rows = jnp.concatenate([z_a, z_b], axis=1)
    kept, *sent = [
        dot32(turned[k * rows_n : (k + 1) * rows_n], z_rows, ((1,), (1,))) for k in range(obs_n)
    ]
    basis = dot32(after(own_rows, sent), inverse, ((1,), (1,))).astype(bf16)
    got = [
        lax.ppermute(part, ("x", "core"), [(i, (i + k) % obs_n) for i in range(obs_n)])
        for k, part in enumerate(sent, 1)
    ]
    laid = jnp.concatenate(got[::-1] + [kept] + got[::-1], axis=1)
    cols_n = kept.shape[1]
    projected = lax.dynamic_slice_in_dim(
        laid, (obs_n - 1 - me) * cols_n, obs_n * cols_n, axis=1
    )
    return (basis, projected)


def solution(mesh):
    obs, par = mesh.shape["obs"], mesh.shape["par"]
    fine = Mesh(mesh.devices.reshape(obs // 2, 2, 4, par // 4), ALL)
    spread = P(ALL)
    placed = (
        P(ALL, None, None),
        P(ALL, None),
        spread,
        spread,
        P(("p", "q"), None),
    )
    return jax.shard_map(
        per_device,
        mesh=fine,
        in_specs=placed,
        out_specs=(P(ALL, None), P(("x", "core"), ("p", "q"))),
        check_vma=False,
    )
```

```python
import functools

import jax
import jax.numpy as jnp
from jax import lax
from jax.experimental import pallas as pl
from jax.experimental.pallas import tpu as pltpu
from jax.sharding import Mesh, PartitionSpec as P

RB_DEV = 32
UNROLL = 32
AHEAD = 2
WAITS = 16
CHUNKS = 2
LEAF = 128
MOST_SLOTS = 512
VMEM_LIMIT = 60 * 1024 * 1024
HIGHEST = lax.Precision.HIGHEST
ALL = ("x", "core", "p", "q")


def shift(value, axis, by):
    size = lax.axis_size(axis)
    return lax.ppermute(value, axis, [(i, (i + by) % size) for i in range(size)])


def swap(value, bits):
    size = lax.axis_size("p")
    return lax.ppermute(value, "p", [(i, i ^ bits) for i in range(size)])


def place_p(here, there):
    differs = here ^ there
    return (differs & 1) * 2 + (differs >> 1)


def gather_p(value, direct=False):
    if direct:
        return jnp.concatenate([value] + [swap(value, bits) for bits in (2, 1, 3)])
    pair = jnp.concatenate([value, swap(value, 2)])
    return jnp.concatenate([pair, swap(pair, 1)])


def reduce_p(total, direct=False):
    f32, bf16 = jnp.float32, jnp.bfloat16
    if direct:
        got = [swap(total[i].astype(bf16), bits) for i, bits in ((1, 2), (2, 1), (3, 3))]
        return sum([part.astype(f32) for part in got], total[0])
    return reduce_rest(reduce_half(total))


def reduce_half(total):
    return total[:2] + swap(total[2:].astype(jnp.bfloat16), 1).astype(jnp.float32)


def reduce_rest(half):
    return half[0] + swap(half[1].astype(jnp.bfloat16), 2).astype(jnp.float32)


def together(*values):
    return lax.optimization_barrier(values)


def after(value, *others):
    return together(value, *others)[0]


def spread_pieces(value, axis):
    return [value] + [shift(value, axis, k) for k in range(1, lax.axis_size(axis))]


def absolute(pieces, axis):
    size, me = len(pieces), lax.axis_index(axis)
    laid = jnp.concatenate(pieces + pieces[:-1], axis=0)
    rows = pieces[0].shape[0]
    return lax.dynamic_slice_in_dim(laid, (size - me) % size * rows, size * rows, axis=0)


def reduce_stage(keep, sends, axis):
    total = keep
    for k, part in enumerate(sends, 1):
        total = total + shift(part, axis, k).astype(jnp.float32)
    return total


def passes_of(bounds):
    groups, room = [], 0
    for i, bound in enumerate(bounds):
        if not groups or room + bound > MOST_SLOTS:
            groups.append([])
            room = 0
        groups[-1].append(i)
        room += bound
    return groups


def slots_of(bounds):
    return max(sum(bounds[i] for i in group) for group in passes_of(bounds))


def list_kernel(counts_in, bounds, spare, rows_ref, cols_ref, counts, index, rows, cols):
    base = [0]
    for held in counts_in:
        base.append(base[-1] + held)
    start = 0
    for group in passes_of(bounds):
        slot = jnp.int32(start)
        for s in group:

            def take(i, slot, s=s):
                row = rows_ref[base[s] + i]

                @pl.when(row >= 0)
                def _():
                    index[slot] = i
                    rows[slot] = row
                    cols[slot] = cols_ref[base[s] + i]

                return slot + jnp.where(row >= 0, 1, 0).astype(jnp.int32)

            before = slot
            slot = lax.fori_loop(0, counts_in[s], take, slot)
            counts[s] = slot - before
        for extra in range(UNROLL - 1):
            rows[slot + extra] = spare
            cols[slot + extra] = 0
        start += sum(bounds[s] for s in group) + UNROLL


def block_lists(counts_in, bounds, spare, rows, cols):
    smem = pl.BlockSpec(memory_space=pltpu.SMEM)
    size = sum(bounds) + UNROLL * len(passes_of(bounds))
    shape = jax.ShapeDtypeStruct((size,), jnp.int32)
    return pl.pallas_call(
        functools.partial(list_kernel, counts_in, bounds, spare),
        out_shape=[jax.ShapeDtypeStruct((len(bounds),), jnp.int32), shape, shape, shape],
        in_specs=[smem, smem],
        out_specs=[smem] * 4,
        cost_estimate=pl.CostEstimate(flops=4 << 30, bytes_accessed=1 << 14, transcendentals=0),
        name="block_lists",
    )(rows, cols)


def accumulate(bounds, contract, lists, sources, panel_copies, scratch):
    counts, index, list_rows, list_cols = lists
    slots, panels, acc, sem, panel_sem = scratch
    copies = [
        pltpu.make_async_copy(source, target, panel_sem.at[i])
        for i, (source, target) in enumerate(panel_copies)
    ]
    for copy in copies:
        copy.start()

    start = 0
    for turn, group in enumerate(passes_of(bounds)):
        count = jnp.int32(0)
        for s in group:

            def take(i, carry, s=s, count=count, start=start):
                slot = count + i
                pltpu.make_async_copy(
                    sources[s].at[index[start + slot]], slots.at[slot], sem
                ).start()
                return carry

            lax.fori_loop(0, counts[s], take, 0)
            count = count + counts[s]
        if turn == 0:

            def clear(i, carry):
                acc[i] = jnp.zeros(acc.shape[1:], acc.dtype)
                return carry

            lax.fori_loop(0, acc.shape[0] - 1, clear, 0)

        def settle(i, carry, n=1):
            some = pl.ds(0, n)
            pltpu.make_async_copy(sources[0].at[some], slots.at[some], sem).wait()
            return carry

        lax.fori_loop(0, count // WAITS, functools.partial(settle, n=WAITS), 0)
        lax.fori_loop(0, count % WAITS, settle, 0)
        if turn == 0:
            for copy in copies:
                copy.wait()

        def step(i, carry, start=start):
            for j in range(UNROLL):
                k = i * UNROLL + j
                row = list_rows[start + k]
                acc[row] += lax.dot_general(
                    slots[k],
                    panels[list_cols[start + k]],
                    (((contract,), (0,)), ((), ())),
                    preferred_element_type=jnp.float32,
                )
            return carry

        lax.fori_loop(0, (count + UNROLL - 1) // UNROLL, step, 0)
        start += sum(bounds[s] for s in group) + UNROLL


def sketch_kernel(bounds, pieces_n, chunk, *refs):
    n = len(bounds)
    lists, sources, pieces = refs[:4], refs[4 : 4 + n], refs[4 + n : 4 + n + pieces_n]
    outs, scratch = refs[4 + n + pieces_n : -5], refs[-5:]
    panels, acc = scratch[1], scratch[2]
    kc = acc.shape[-1]
    copies, base = [], 0
    for piece in pieces:
        rows = piece.shape[0]
        copies.append((piece.at[:, :, pl.ds(chunk * kc, kc)], panels.at[pl.ds(base, rows)]))
        base += rows
    accumulate(bounds, 1, lists, sources, copies, scratch)
    per = outs[0].shape[0]
    outs = outs[-((acc.shape[0] - 1) // per) :]
    for g, out in enumerate(outs):

        def give(i, carry, g=g, out=out):
            out[i] = acc[g * per + i].astype(out.dtype)
            return carry

        lax.fori_loop(0, per, give, 0)


def project_kernel(bounds, pieces_n, x_n, q_n, *refs):
    n = len(bounds)
    lists, sources, pieces = refs[:4], refs[4 : 4 + n], refs[4 + n : 4 + n + pieces_n]
    outs, scratch = refs[4 + n + pieces_n : -5], refs[-5:]
    panels, acc = scratch[1], scratch[2]
    copies, base = [], 0
    for piece in pieces:
        rows = piece.shape[0]
        copies.append((piece, panels.at[pl.ds(base, rows)]))
        base += rows
    accumulate(bounds, 0, lists, sources, copies, scratch)
    width = acc.shape[-1] // 2
    inner = (acc.shape[0] - 1) // (x_n * q_n)
    for g in range(x_n):

        def give_x(i, carry, g=g):
            out = outs[g]
            out[i] = acc[g * q_n * inner + i, :, :width].astype(out.dtype)
            return carry

        lax.fori_loop(0, q_n * inner, give_x, 0)
    for g in range(q_n):
        for x in range(x_n):

            def give_q(i, carry, g=g, x=x):
                out = outs[x_n + g]
                out[x * inner + i] = acc[(x * q_n + g) * inner + i, :, width:].astype(out.dtype)
                return carry

            lax.fori_loop(0, inner, give_q, 0)


def block_products(kernel, bounds, lists, sources, pieces, acc_n, width, outs, name, late=()):
    wide = sources[0].shape[1]
    smem = pl.BlockSpec(memory_space=pltpu.SMEM)
    anywhere = pl.BlockSpec(memory_space=pl.ANY)
    return pl.pallas_call(
        kernel,
        out_shape=outs,
        in_specs=[smem] * 4 + [anywhere] * (len(sources) + len(pieces) + len(late)),
        out_specs=[pl.BlockSpec(memory_space=pltpu.VMEM)] * len(outs),
        scratch_shapes=[
            pltpu.VMEM((slots_of(bounds) + UNROLL, wide, wide), jnp.bfloat16),
            pltpu.VMEM((sum(p.shape[0] for p in pieces), wide, width), jnp.bfloat16),
            pltpu.VMEM((acc_n + 1, wide, width), jnp.float32),
            pltpu.SemaphoreType.DMA,
            pltpu.SemaphoreType.DMA((len(pieces),)),
        ],
        compiler_params=pltpu.CompilerParams(vmem_limit_bytes=VMEM_LIMIT),
        cost_estimate=pl.CostEstimate(
            flops=2 * 128 * wide * wide * width, bytes_accessed=32 << 20, transcendentals=0
        ),
        name=name,
    )(*lists, *sources, *pieces, *late)


def dot32(a, b, dims):
    return lax.dot_general(
        a, b, (dims, ((), ())), precision=HIGHEST, preferred_element_type=jnp.float32
    )


def leaf_inverse(a):
    n = a.shape[0]
    place = lax.broadcasted_iota(jnp.int32, (n, n), 0)
    lane = lax.broadcasted_iota(jnp.int32, (n, n), 1)
    unit = jnp.where(place == lane, 1.0, 0.0).astype(a.dtype)
    pivots = jnp.ones((n, n), a.dtype)
    columns = {j: jnp.broadcast_to(a[:, j : j + 1], (n, n)) for j in range(AHEAD + 1)}
    for j in range(n):
        column = columns.pop(j)
        pivot = column[j : j + 1]
        times = jnp.where(place > j, column * (1.0 / pivot), 0.0)
        pivots = jnp.where(place == j, pivot, pivots)
        for t in columns:
            columns[t] = columns[t] - times * column[t : t + 1]
        a, unit = a - times * a[j : j + 1], unit - times * unit[j : j + 1]
        t = j + AHEAD + 1
        if t < n:
            columns[t] = jnp.broadcast_to(a[:, t : t + 1], (n, n))
    return unit * lax.rsqrt(pivots)


def gram_kernel(n, core_ref, *refs):
    out = refs[-1]
    rows_n = out.shape[0]

    @pl.when(pl.program_id(0) == 0)
    def _():
        out[...] = jnp.zeros(out.shape, out.dtype)

    first_row = 0 if rows_n == refs[0].shape[1] else pl.multiple_of(core_ref[0] * rows_n, rows_n)
    some = pl.ds(first_row, rows_n)
    for first in range(0, len(refs) - 1, n):
        at = first // n * refs[0].shape[1]
        total = out[:, at : at + refs[0].shape[1]]
        for mine, other in zip(refs[-1 - n : -1], refs[first : first + n]):
            total += lax.dot_general(
                mine[:, some], other[...], (((0,), (0,)), ((), ())),
                preferred_element_type=jnp.float32,
            )
        out[:, at : at + refs[0].shape[1]] = total


def gram_rows(core, chunks, rows_n):
    n = len(chunks[-1])
    rows, cols = chunks[-1][0].shape
    steps = 4
    parts = [part for chunk in chunks for part in chunk]
    return pl.pallas_call(
        functools.partial(gram_kernel, n),
        grid=(steps,),
        out_shape=jax.ShapeDtypeStruct((rows_n, cols * len(chunks)), jnp.float32),
        in_specs=[pl.BlockSpec(memory_space=pltpu.SMEM)]
        + [pl.BlockSpec((rows // steps, cols), lambda i: (i, 0))] * len(parts),
        out_specs=pl.BlockSpec((rows_n, cols * len(chunks)), lambda i: (0, 0)),
        compiler_params=pltpu.CompilerParams(vmem_limit_bytes=24 << 20),
        cost_estimate=pl.CostEstimate(flops=2 << 30, bytes_accessed=8 << 20, transcendentals=0),
        name="gram_rows",
    )(core, *parts)


def inverse_kernel(scale, k, first, gram, *refs):
    before, out = refs[:k], refs[-1]
    n = out.shape[0]
    grams = [gram[first : first + n, j * n : (j + 1) * n] * scale for j in range(k + 1)]
    rest = grams[k]
    factors = []
    for j in range(k):
        factor = dot32(grams[0], before[j][:, :n], ((1,), (1,)))
        for i in range(1, j + 1):
            factor += dot32(grams[i], before[j][:, i * n : (i + 1) * n], ((1,), (1,)))
        rest = rest - dot32(factor, factor, ((1,), (1,)))
        factors.append(factor)
    corner = leaf_inverse(rest)
    out[...] = jnp.zeros(out.shape, out.dtype)
    if k:
        total = dot32(factors[0], before[0][:, : k * n], ((1,), (0,)))
        for j in range(1, k):
            total += dot32(factors[j], before[j][:, : k * n], ((1,), (0,)))
        out[:, : k * n] = -dot32(corner, total, ((1,), (0,)))
    out[:, k * n : (k + 1) * n] = corner


def inverse_rows(scale, gram, first, before, width, late):
    vmem, anywhere = pl.BlockSpec(memory_space=pltpu.VMEM), pl.BlockSpec(memory_space=pl.ANY)
    return pl.pallas_call(
        functools.partial(inverse_kernel, scale, len(before), first),
        out_shape=jax.ShapeDtypeStruct((LEAF, width), jnp.float32),
        in_specs=[vmem] * (1 + len(before)) + [anywhere] * len(late),
        out_specs=vmem,
        compiler_params=pltpu.CompilerParams(vmem_limit_bytes=16 << 20),
        cost_estimate=pl.CostEstimate(flops=1 << 26, bytes_accessed=1 << 16, transcendentals=0),
        name="inverse_rows",
    )(gram, *before, *late)


def per_device(blocks, owner, row_local, col_local, sketch):
    x_n, q_n, p_n = lax.axis_size("x"), lax.axis_size("q"), lax.axis_size("p")
    xi, ci, zi, yi = (lax.axis_index(a) for a in ALL)
    par = p_n * q_n
    total_devs = 2 * x_n * par
    held, wide = blocks.shape[0], blocks.shape[1]
    width = sketch.shape[1]
    col_dev = sketch.shape[0] // wide
    slot_cap = max(2, (2 * held + total_devs - 1) // total_devs)
    rows_each = RB_DEV // par
    cols_each = col_dev // (2 * x_n)
    all_rows = RB_DEV * wide * 2 * x_n
    bf16, f32 = jnp.bfloat16, jnp.float32
    kc = width // CHUNKS
    by_q_n = held // 4
    by_x_n = held - by_q_n

    first, last = blocks[:by_q_n], blocks[by_x_n:]
    half = col_dev // 2
    early_n = half // 2
    later_n = half - early_n
    panels = sketch.reshape(col_dev, wide, width)
    mine = lax.dynamic_slice_in_dim(panels, ci * half, half, axis=0)
    code = (owner[:, 0] * RB_DEV + row_local) * col_dev + col_local

    def along_x(value):
        return [shift(value, "x", k) for k in range(1, x_n)]

    def along_q(value):
        return [shift(value, "q", k) for k in range(1, q_n)]

    def across(values):
        return [shift(value, "core", 1) for value in values]

    code_x, code_q, (code_far,) = along_x(code), along_q(code), across([code])
    first, code_x = together(first, code_x)
    last, code_q = together(last, code_q)
    line, got_0, got_q, (sibling,), code_far, mine, second = together(
        gather_p(mine[:early_n]), along_x(first), along_q(last), across([blocks]),
        code_far, mine, after(blocks, code_far)[by_q_n : 2 * by_q_n],
    )
    third = after(blocks, second)[2 * by_q_n : by_x_n]
    early = [line] + along_q(line)
    line, early, got_1, far_0, far_q, code_x_far, code_q_far, third = together(
        gather_p(mine[early_n:]), early, along_x(second), across(got_0), across(got_q),
        across(code_x), across(code_q), third,
    )
    later = [line] + along_q(line)

    codes, along = [code, code_far], [jnp.arange(held) < by_x_n] * 2
    for i in range(3):
        for near, far in zip(code_x, code_x_far):
            codes += [c[i * by_q_n : (i + 1) * by_q_n] for c in (near, far)]
            along += [jnp.ones((by_q_n,), bool)] * 2
    for near, far in zip(code_q, code_q_far):
        codes += [near[by_x_n:], far[by_x_n:]]
        along += [jnp.zeros((by_q_n,), bool)] * 2
    counts = [c.shape[0] for c in codes]
    most_y, most_p = min(by_x_n, par * slot_cap), min(by_x_n, 2 * par * slot_cap)
    thirds = 6 * (x_n - 1)
    bounds_y = [most_y + by_q_n] * 2 + [min(by_q_n, most_y)] * thirds + [by_q_n] * (2 * q_n - 2)
    bounds_p = [most_p + by_q_n] * 2 + [min(by_q_n, most_p)] * thirds + [by_q_n] * (2 * q_n - 2)
    codes, along = jnp.concatenate(codes), jnp.concatenate(along)

    owners = codes // (RB_DEV * col_dev)
    row = codes // col_dev % RB_DEV
    col = codes % col_dev
    o_obs, o_par = owners // par, owners % par
    o_x, o_core = o_obs // 2, o_obs % 2
    o_z, o_y = o_par // q_n, o_par % q_n
    r_par, r_in = row // rows_each, row % rows_each
    r_z, r_y = r_par // q_n, r_par % q_n
    c_x, c_core, c_in = col // (2 * cols_each), col // cols_each % 2, col % cols_each

    per = p_n * rows_each
    groups = q_n + x_n - 1
    other_x = q_n - 1 + (o_x - xi) % x_n
    y_group = jnp.where(along, (r_y - yi) % q_n, jnp.where(o_x == xi, 0, other_x))
    y_slot = (y_group * p_n + place_p(zi, r_z)) * rows_each + r_in
    y_mine = (o_core == ci) & jnp.where(along, o_x == xi, r_y == yi)
    y_slot = jnp.where(y_mine, y_slot, -1)
    place = col % half
    device = (yi - o_y) % q_n * p_n + place_p(zi, o_z)
    y_panel = jnp.where(
        place < early_n,
        device * early_n + place,
        2 * par * early_n + device * later_n + place - early_n,
    )
    other = jnp.where(place < early_n, par * early_n, par * later_n)
    y_panel = y_panel + jnp.where(col // half == ci, 0, other)

    p_slot = ((c_x - xi) % x_n * q_n + (o_y - yi) % q_n) * p_n + place_p(zi, o_z)
    p_slot = p_slot * cols_each + c_in
    p_mine = (c_core == ci) & jnp.where(along, o_x == xi, r_y == yi)
    p_slot = jnp.where(p_mine, p_slot, -1)
    in_part = place_p(zi, r_z) * rows_each + r_in
    y_part = jnp.where(o_x == xi, (yi - r_y) % q_n, q_n - 1 + (xi - o_x) % x_n)
    p_panel = (jnp.where(o_core == ci, 0, groups) + y_part) * per + in_part
    slots = x_n * q_n * p_n * cols_each
    lists_y = block_lists(counts, bounds_y, groups * per, y_slot, y_panel)
    lists_p = block_lists(counts, bounds_p, slots, p_slot, p_panel)
    later, early_far, got_2, far_1, lists_y, lists_p = together(
        later, across(early), along_x(third), across(got_1), lists_y, lists_p
    )
    later_far, far_2 = across(later), across(got_2)
    sketch_pieces = early + early_far + later + later_far
    sources = [blocks, sibling]
    for gots, fars in ((got_0, far_0), (got_1, far_1), (got_2, far_2), (got_q, far_q)):
        for got, far in zip(gots, fars):
            sources += [got, far]

    def y_products(chunk, late):
        shapes = [
            jax.ShapeDtypeStruct((per, wide, kc), bf16 if g else f32) for g in range(groups)
        ]
        return block_products(
            functools.partial(sketch_kernel, bounds_y, len(sketch_pieces), chunk), bounds_y,
            lists_y, sources, sketch_pieces, groups * per, kc, shapes, "sketch_products", late,
        )

    def y_received(parts):
        return (
            [shift(parts[k], "q", k) for k in range(1, q_n)]
            + [shift(parts[q_n - 1 + k], "x", k) for k in range(1, x_n)]
        )

    def y_summed(parts, got, direct):
        keep = parts[0]
        for part in got:
            keep = keep + part.astype(f32)
        return reduce_p(keep.reshape(p_n, rows_each * wide, kc), direct)

    def spread(line):
        return (
            [shift(line, "q", k) for k in range(1, q_n)],
            [shift(line, "x", k) for k in range(1, x_n)],
        )

    def same_x(parts):
        return parts[:q_n] + parts[groups : groups + q_n]

    def z_products(parts):
        kh = kc // 2
        shapes = [
            jax.ShapeDtypeStruct((slots // n, wide, kh), f32 if k == 0 else bf16)
            for n in (x_n, q_n) for k in range(n)
        ]
        pieces = [a.reshape(-1, wide, kc) for a in parts]
        return block_products(
            functools.partial(project_kernel, bounds_p, len(pieces), x_n, q_n), bounds_p,
            lists_p, sources, pieces, slots, kc, shapes, "project_products",
        )

    def z_first(parts):
        return (
            [shift(parts[k], "x", k) for k in range(1, x_n)],
            [shift(parts[x_n + k], "q", k) for k in range(1, q_n)],
        )

    def z_summed(parts, got):
        by_x, by_q = parts[0], parts[x_n]
        for part in got[0]:
            by_x = by_x + part.astype(f32)
        for part in got[1]:
            by_q = by_q + part.astype(f32)
        return (
            by_x.reshape(q_n, p_n, cols_each * wide, kc // 2),
            by_q.reshape(x_n, p_n, cols_each * wide, kc // 2),
        )

    def z_second(by_x, by_q):
        by_x = reduce_stage(by_x[0], [by_x[k].astype(bf16) for k in range(1, q_n)], "q")
        by_q = reduce_stage(by_q[0], [by_q[k].astype(bf16) for k in range(1, x_n)], "x")
        return jnp.concatenate([by_x, by_q], axis=2)

    inverse = []

    def more_rows(gram, *late):
        inverse.append(
            inverse_rows(
                1.0 / all_rows, gram, len(inverse) * LEAF % kc, inverse, width, late
            )
        )
        return inverse[-1]

    core = jnp.reshape(ci, (1,)).astype(jnp.int32)
    parts_a = y_products(0, ())
    got_a = y_received(parts_a)
    got_a, parts_b = together(got_a, y_products(1, (parts_a[0],)))
    got_b = y_received(parts_b)
    own_a, got_b = together(y_summed(parts_a, got_a, True), got_b)
    line_a, own_b = together(gather_p(own_a.astype(bf16)), y_summed(parts_b, got_b, False))
    line_b, spread_a = together(gather_p(own_b.astype(bf16), True), spread(line_a))
    spread_b = spread(line_b)
    all_a = [line_a, *spread_a[0], *spread_a[1]]
    all_a = together(all_a + across(all_a))[0]
    near_a = same_x(all_a)
    line_b_far, spread_b, zs_a, gram_a = together(
        across([line_b]), spread_b, z_products(all_a), gram_rows(core, [near_a], kc)
    )

    first_a = z_first(zs_a)
    got_gram = along_x(gram_a)
    spread_b = spread_b[0] + spread_b[1]
    all_b = together([line_b, *spread_b, *line_b_far, *across(spread_b)])[0]
    gram_b = gram_rows(core, [near_a, same_x(all_b)], kc // 2)
    got_b = along_x(gram_b)
    first_a, zs_b, got_b = together(first_a, z_products(after(all_b, gram_b)), got_b)
    first_b = z_first(zs_b)
    gram_b = sum(got_b, gram_b)
    gram_b = absolute([gram_b, shift(gram_b, "core", 1)], "core")
    gram_a = sum(after(got_gram, zs_b), gram_a)
    second_a = z_second(*z_summed(zs_a, first_a))
    more_rows(gram_a, zs_b[0])
    more_rows(gram_a)
    first_b, gram_b, _ = together(first_b, gram_b, inverse[-1])
    summed_b = z_summed(zs_b, first_b)
    second_b = z_second(*summed_b)
    z_a = reduce_p(after(second_a, summed_b))
    more_rows(gram_b, summed_b[0])
    second_b, _ = together(second_b, inverse[-1])
    half_b = reduce_half(second_b)
    more_rows(gram_b, second_b)
    half_b, _ = together(half_b, inverse[-1])
    z_b = reduce_rest(half_b)
    inverse = jnp.concatenate(inverse, axis=0)
    own_rows = jnp.concatenate([own_a, own_b], axis=1)

    obs_n, me = 2 * x_n, xi * 2 + ci
    rows_n = width // obs_n
    turned = jnp.concatenate([inverse, inverse[:-rows_n]], axis=0)
    turned = lax.dynamic_slice_in_dim(turned, me * rows_n, width, axis=0)
    z_rows = jnp.concatenate([z_a, z_b], axis=1)
    kept, *sent = [
        dot32(turned[k * rows_n : (k + 1) * rows_n], z_rows, ((1,), (1,))) for k in range(obs_n)
    ]
    sent = [part.astype(bf16) for part in sent]
    basis = dot32(after(own_rows, sent), inverse, ((1,), (1,))).astype(bf16)
    got = [
        lax.ppermute(part, ("x", "core"), [(i, (i + k) % obs_n) for i in range(obs_n)]).astype(f32)
        for k, part in enumerate(sent, 1)
    ]
    laid = jnp.concatenate(got[::-1] + [kept] + got[::-1], axis=1)
    cols_n = kept.shape[1]
    projected = lax.dynamic_slice_in_dim(
        laid, (obs_n - 1 - me) * cols_n, obs_n * cols_n, axis=1
    )
    return (basis, projected)


def solution(mesh):
    obs, par = mesh.shape["obs"], mesh.shape["par"]
    fine = Mesh(mesh.devices.reshape(obs // 2, 2, 4, par // 4), ALL)
    spread = P(ALL)
    placed = (
        P(ALL, None, None),
        P(ALL, None),
        spread,
        spread,
        P(("p", "q"), None),
    )
    return jax.shard_map(
        per_device,
        mesh=fine,
        in_specs=placed,
        out_specs=(P(ALL, None), P(("x", "core"), ("p", "q"))),
        check_vma=False,
    )
```
